32 devices in a mesh: groups: 2 (over y), row: 2 (over x), col: 4 (over z), rep: 2 (over core).
Axes of the slice: x: 2, y: 2, z: 4, core: 2. Of those that a mesh axis runs over, the one named last changes fastest.
Arguments:
- left_features: bfloat16 [32, 8192], P(('groups', 'row', 'col'), 'rep'), parts along dimension 0, may hold values from -6 to 6
- right_features: bfloat16 [32, 8192], P(('groups', 'col', 'row'), 'rep'), parts along dimension 0, may hold values from -6 to 6
- weight: bfloat16 [1024, 128], replicated, may hold values from -3 to 3
- bias: float32 [128], replicated, may hold values from -4 to 4
- cotangent: bfloat16 [32, 16, 128], P(('groups', 'row'), 'col'), parts along dimension 0, may hold values from -0.59765625 to 0.59765625
Outputs:
- pair_out: float32 [32, 16, 128], P(('groups', 'row'), ('col', 'rep')), parts along dimension 0
- left_grad: bfloat16 [32, 8192], P(('groups', 'row', 'col'), 'rep'), parts along dimension 0
- right_grad: bfloat16 [32, 8192], P(('groups', 'col', 'row'), 'rep'), parts along dimension 0
- weight_grad: float32 [2048, 128], P('groups'), parts along dimension 0
The draws below stay inside these ranges and needn't reach their ends.
There are 2 independent parts, one for each index of `groups`. The reference program is written for one: setup_inputs(seed, part) draws one part's arguments, and reference() takes and returns one part's arrays. A program takes and returns all parts, laid end to end along the dimension named above; an argument that names none is the same for every part. Nothing has to cross between parts.
All inputs are finite; a program needn't handle non-finite values.
Results may differ from the reference program's by a relative error of at most 0.0049.
Values may be sent and summed in bfloat16 or wider, within the bound.
No kernel may reach another device: no remote copies, remote signals or barrier semaphores. Data moves between devices by JAX's collectives and lax.ppermute only.
A program may use at most 64 MiB of HBM per device.

```python
import jax
import jax.numpy as jnp
from jax import lax

C = 32
E = 128
S = 256
L = 16
N_ROW = 2


def block_scale(stream_key, extent, shards, least, high):
    def one(axis_at, shards_of):
        steps = jax.random.uniform(jax.random.fold_in(jax.random.fold_in(stream_key, 6), axis_at), (shards_of,), jnp.float32, least / len(shards), high / len(shards))
        return jnp.repeat(jnp.exp(steps), extent[axis_at] // shards_of).reshape((-1,) + (1,) * (len(extent) - axis_at - 1))

    gain = one(*shards[0])
    for cut in shards[1:]:
        gain = gain * one(*cut)
    return gain


def gaussian(own_key, shape, spread, reach, shards=(), held_as=jnp.bfloat16):
    drawn = jax.random.normal(own_key, shape, jnp.float32) * spread
    if len(shards) > 0:
        drawn = block_scale(own_key, shape, shards, -0.22, 0.18) * drawn
    return jnp.clip(drawn, min=-reach, max=reach).astype(held_as)


def setup_inputs(seed: int = 0, part: int = 0) -> dict:
    seeds = jax.random.split(jax.random.key(seed), 6)
    part_splits = jax.random.split(jax.random.fold_in(seeds[5], part), 6)
    return {
        "left_features": gaussian(part_splits[0], (L, S * C), 1.0, 6.0, ((0, 8), (1, 2))),
        "right_features": gaussian(part_splits[1], (L, S * C), 1.0, 6.0, ((0, 8), (1, 2))),
        "weight": gaussian(seeds[2], (C * C, E), (C * C // S) ** -0.5, 3.0),
        "bias": gaussian(seeds[3], (E,), 1.0, 4.0, (), jnp.float32),
        "cotangent": gaussian(part_splits[4], (L, L, E), 0.1, 0.59765625, ((0, 2), (1, 4))),
    }


def reference(left_features, right_features, weight, bias, cotangent):
    half_seqs = S // 2
    left_all = left_features.reshape(L, S, C).astype(jnp.float32)
    right_all = right_features.reshape(L, S, C).astype(jnp.float32)
    row_block = L // N_ROW

    def step_fn(carried, block_index):
        right_acc, weight_acc = carried
        first_row = (block_index * row_block).astype(jnp.int32)
        left_rows = lax.dynamic_slice_in_dim(left_all, first_row, row_block, 0)
        grad_rows = lax.dynamic_slice_in_dim(cotangent, first_row, row_block, 0).reshape(row_block * L, E)
        pair_total = jnp.zeros((row_block * L, E), jnp.float32)
        for lower in (0, half_seqs):
            outer_sum = jnp.einsum("isc,jsd->ijcd", left_rows[:, lower:lower + half_seqs], right_all[:, lower:lower + half_seqs])
            half_mean = (outer_sum / S).astype(jnp.bfloat16).reshape(row_block * L, C * C)
            pair_total = pair_total + jnp.dot(half_mean, weight, preferred_element_type=jnp.float32)
            weight_acc = weight_acc + jnp.dot(half_mean.T, grad_rows, preferred_element_type=jnp.float32)
        pair_out = (pair_total + bias).astype(jnp.float32).reshape(row_block, L, E)
        grad_mean = (jnp.dot(grad_rows, weight.T, preferred_element_type=jnp.float32) / S).astype(jnp.bfloat16)
        grad_mean = grad_mean.reshape(row_block, L, C, C).astype(jnp.float32)
        left_grad = jnp.einsum("ijcd,jsd->isc", grad_mean, right_all).astype(jnp.bfloat16).reshape(row_block, S * C)
        right_acc = right_acc + jnp.einsum("ijcd,isc->jsd", grad_mean, left_rows)
        return (right_acc, weight_acc), (pair_out, left_grad)

    initial = (jnp.zeros((L, S, C), jnp.float32), jnp.zeros((C * C, E), jnp.float32))
    (right_acc, weight_acc), (pair_blocks, left_blocks) = lax.scan(step_fn, initial, jnp.arange(N_ROW, dtype=jnp.int32))
    pair_out = pair_blocks.reshape(L, L, E)
    left_grad = left_blocks.reshape(L, S * C)
    right_grad = right_acc.astype(jnp.bfloat16).reshape(L, S * C)
    return (pair_out, left_grad, right_grad, weight_acc)
```

```python
import functools

import jax
import jax.numpy as jnp
from jax import lax
from jax.experimental import pallas as pl
from jax.experimental.pallas import tpu as pltpu
from jax.sharding import PartitionSpec as P

C = 32
S = 256
LANES = 128
F32 = jnp.float32
BF16 = jnp.bfloat16
NT = (((1,), (1,)), ((), ()))


def tile_plan(left_features, right_features, weight, bias, cotangent):
    left_rows = lax.all_gather(left_features, "col", axis=0, tiled=True)
    right_rows = lax.all_gather(right_features, "row", axis=0, tiled=True)
    row_count = left_rows.shape[0]
    col_count = right_rows.shape[0]
    out_width = weight.shape[1]
    left_block = left_rows.reshape(row_count, -1, C)
    right_block = right_rows.reshape(col_count, -1, C)
    outer_sum = jnp.einsum(
        "isc,jsd->ijcd", left_block, right_block, preferred_element_type=jnp.float32
    )
    half_mean = (outer_sum / S).astype(jnp.bfloat16).reshape(row_count * col_count, C * C)
    proj_part = jnp.dot(half_mean, weight, preferred_element_type=jnp.float32).reshape(
        row_count, col_count, out_width
    )
    pair_sum = lax.psum_scatter(proj_part, "rep", scatter_dimension=1, tiled=True)
    pair_out = pair_sum + bias
    flat_grad = cotangent.reshape(row_count * col_count, out_width)
    weight_part = jnp.einsum("pk,pe->ke", half_mean, flat_grad, preferred_element_type=jnp.float32)
    weight_grad = lax.psum(weight_part, ("row", "col", "rep"))
    grad_mean = jnp.einsum("pe,ke->pk", flat_grad, weight, preferred_element_type=jnp.float32) / S
    grad_mean = grad_mean.astype(jnp.bfloat16).reshape(row_count, col_count, C, C)
    left_part = jnp.einsum(
        "ijcd,jsd->isc", grad_mean, right_block, preferred_element_type=jnp.float32
    ).reshape(row_count, -1)
    right_part = jnp.einsum(
        "ijcd,isc->jsd", grad_mean, left_block, preferred_element_type=jnp.float32
    ).reshape(col_count, -1)
    left_sum = lax.psum_scatter(left_part, "col", scatter_dimension=0, tiled=True)
    right_sum = lax.psum_scatter(right_part, "row", scatter_dimension=0, tiled=True)
    return (pair_out, left_sum.astype(jnp.bfloat16), right_sum.astype(jnp.bfloat16), weight_grad)


def exchange(x, axis, flip, size):
    return lax.ppermute(x, axis, [(k, k ^ flip) for k in range(size)])


def sort_kernel(rows, cols, where, near, far, feats, cot, scratch):
    tokens = 2 * rows * cols
    span = tokens * C
    my_row, my_col = where[0], where[1]
    for half, block in enumerate((near, far)):
        for slot in range(cols):
            row = lax.rem(my_row + half, rows)
            col = my_col ^ slot
            left_token = (row * cols + col) * 2
            for t in range(2):
                scratch[pl.ds(left_token + t, C, stride=tokens), :] = block[slot, t * C:(t + 1) * C, :].astype(F32)
            right_at = pl.multiple_of(span + (col * rows + row) * 2 * C, 2 * C)
            feats[pl.ds(right_at, 2 * C), :] = block[slot, 2 * C:4 * C, :]
            per_row, per_col = tokens // rows, tokens // cols
            for j in range(per_col):
                at = pl.multiple_of((col * per_col + j) * tokens + row * per_row, per_row)
                first = 4 * C + j * per_row
                cot[pl.ds(at, per_row), :] = block[slot, first:first + per_row, :].astype(F32)
    feats[:span, :] = scratch[...].astype(BF16)


def feature_grad(outer_weight, cot_rows, features, tokens):
    copies = LANES // tokens
    repeated = jnp.concatenate([jnp.concatenate([rows] * copies, axis=0) for rows in cot_rows], axis=0).astype(BF16)
    grads = lax.dot_general(outer_weight, repeated, NT, preferred_element_type=F32)
    copy_of = lax.broadcasted_iota(jnp.int32, (C, LANES), 1) // tokens
    out = []
    for two in range(2):
        lanes = grads[:, two * LANES:(two + 1) * LANES]
        parts = []
        for group in range(C // copies):
            first = group * copies * C
            part = lanes[first:first + C, :]
            for k in range(1, copies):
                at = first + k * C
                part = jnp.where(copy_of == k, lanes[at:at + C, :], part)
            parts.append((part * (1.0 / S)).astype(BF16))
        out.append(jnp.concatenate(parts, axis=1))
    return jnp.dot(jnp.concatenate(out, axis=0), features, preferred_element_type=F32)


def grads_kernel(rows, cols, where, feats, cot, weight, weight_dc, left_grad, right_grad, scratch):
    tokens = 2 * rows * cols
    span = tokens * C
    my_row, my_col = where[0], where[1]
    for j in range(tokens):
        at = span + j * C
        scratch[pl.ds(j, C, stride=tokens), :] = feats[at:at + C, :].astype(F32)
    left_token = (my_row * cols + my_col) * 2
    cot_rows = [cot[pl.ds(left_token + t, tokens, stride=tokens), :] for t in range(2)]
    left_grad[...] = feature_grad(weight_dc[...], cot_rows, scratch[...].astype(BF16), tokens)
    right_token = (my_col * rows + my_row) * 2
    cot_rows = [cot[pl.ds(pl.multiple_of((right_token + t) * tokens, tokens), tokens), :] for t in range(2)]
    right_grad[...] = feature_grad(weight[...], cot_rows, feats[:span, :], tokens)


def swap_blocks(blocks, width):
    count = len(blocks)
    lane_block = lax.broadcasted_iota(jnp.int32, blocks[0].shape, 1) // width
    bit = 1
    while bit < count:
        upper = (lane_block & bit) != 0
        out = list(blocks)
        for a in range(count):
            if a & bit == 0:
                low, high = blocks[a], blocks[a | bit]
                out[a] = jnp.where(upper, pltpu.roll(high, bit * width, 1), low)
                out[a | bit] = jnp.where(upper, high, pltpu.roll(low, LANES - bit * width, 1))
        blocks = out
        bit *= 2
    return blocks


def outer_kernel(rows, cols, where, own, other, cot, weight_t, bias, pair_out, weight_grad, scratch, pair_scratch):
    tokens = 2 * rows * cols
    span = tokens * C
    my_row, my_col, my_rep = where[0], where[1], where[2]
    scratch[my_rep] = own[...]
    scratch[1 - my_rep] = other[...]
    count = LANES // tokens
    right = jnp.concatenate([scratch[0, span:, :], scratch[1, span:, :]], axis=1)
    cot_all = cot[...].astype(BF16)
    pair_t = jnp.zeros((weight_t.shape[0], tokens * tokens), F32)
    for g in range(C // count):
        lanes = slice(g * LANES, (g + 1) * LANES)
        left = jnp.concatenate([scratch[0, lanes, :], scratch[1, lanes, :]], axis=1)
        outer = lax.dot_general(right, left, NT, preferred_element_type=F32) * (1.0 / S)
        parts = []
        for h in range(tokens // count):
            first = h * count * C
            blocks = [outer[first + k * C:first + (k + 1) * C, :] for k in range(count)]
            parts.append(jnp.concatenate(swap_blocks(blocks, tokens), axis=0).astype(BF16))
        mean = jnp.concatenate(parts, axis=1)
        at = slice(g * count * C, (g + 1) * count * C)
        weight_grad[at, :] = jnp.dot(mean, cot_all, preferred_element_type=F32)
        pair_t += jnp.dot(weight_t[:, at], mean, preferred_element_type=F32)
    pair_scratch[...] = pair_t.T
    per_row, per_col = tokens // rows, tokens // cols
    for j in range(per_col // 2):
        col = my_col * per_col + my_rep * (per_col // 2) + j
        at = pl.multiple_of(col * tokens + my_row * per_row, per_row)
        pair_out[:, j, :] = pair_scratch[pl.ds(at, per_row), :] + bias[...]


def gather_plan(rows, cols, left_features, right_features, weight, bias, cotangent):
    held, width = left_features.shape
    seqs = width // C
    tokens = held * rows * cols
    span = tokens * C
    e = weight.shape[1]
    vmem = pl.BlockSpec(memory_space=pltpu.VMEM)
    smem = pl.BlockSpec(memory_space=pltpu.SMEM)
    params = pltpu.CompilerParams(vmem_limit_bytes=32 * 1024 * 1024)
    where = jnp.stack([lax.axis_index("row"), lax.axis_index("col"), lax.axis_index("rep")]).astype(jnp.int32)

    def turned(x):
        return x.reshape(held, seqs, C).transpose(0, 2, 1).reshape(held * C, seqs)

    cot_block = cotangent.transpose(1, 0, 2).reshape(-1, e)
    block = jnp.concatenate([turned(left_features), turned(right_features), cot_block], axis=0)[None]
    flip = 1
    while flip < cols:
        block = jnp.concatenate([block, exchange(block, "col", flip, cols)], axis=0)
        flip *= 2
    far = exchange(block, "row", 1, rows)

    feats, cot = pl.pallas_call(
        functools.partial(sort_kernel, rows, cols),
        out_shape=(
            jax.ShapeDtypeStruct((2 * span, seqs), BF16),
            jax.ShapeDtypeStruct((tokens * tokens, e), F32),
        ),
        in_specs=[smem, vmem, vmem],
        out_specs=(vmem, vmem),
        scratch_shapes=[pltpu.VMEM((span, seqs), F32)],
        compiler_params=params,
        name="sort_tokens",
    )(where, block, far)
    other = exchange(feats, "rep", 1, 2)

    weight_dc = weight.reshape(C, C, e).transpose(1, 0, 2).reshape(C * C, e)
    left_grad, right_grad = pl.pallas_call(
        functools.partial(grads_kernel, rows, cols),
        out_shape=(jax.ShapeDtypeStruct((held * C, seqs), F32),) * 2,
        in_specs=[smem] + [vmem] * 4,
        out_specs=(vmem, vmem),
        scratch_shapes=[pltpu.VMEM((span, seqs), F32)],
        compiler_params=params,
        name="feature_grads",
    )(where, feats, cot, weight, weight_dc)

    pair_out, weight_grad = pl.pallas_call(
        functools.partial(outer_kernel, rows, cols),
        out_shape=(
            jax.ShapeDtypeStruct((tokens // rows, tokens // cols // 2, e), F32),
            jax.ShapeDtypeStruct((C * C, e), F32),
        ),
        in_specs=[smem] + [vmem] * 5,
        out_specs=(vmem, vmem),
        scratch_shapes=[pltpu.VMEM((2, 2 * span, seqs), BF16), pltpu.VMEM((tokens * tokens, e), F32)],
        compiler_params=params,
        name="outer_mean",
    )(where, feats, other, cot, weight.T, bias.reshape(1, e))

    def turned_back(x):
        return x.reshape(held, C, seqs).transpose(0, 2, 1).reshape(held, width).astype(BF16)

    return pair_out, turned_back(left_grad), turned_back(right_grad), weight_grad


def solution(mesh):
    rows, cols = mesh.shape["row"], mesh.shape["col"]

    def on_device(left_features, right_features, weight, bias, cotangent):
        held, width = left_features.shape
        tokens = held * rows * cols
        small = held == 2 and rows == 2 and cols & (cols - 1) == 0 and LANES % tokens == 0 and tokens % 16 == 0
        if small and width == LANES * C and weight.shape[1] == LANES and C % (LANES // tokens) == 0:
            return gather_plan(rows, cols, left_features, right_features, weight, bias, cotangent)
        return tile_plan(left_features, right_features, weight, bias, cotangent)

    in_specs = (
        P(("groups", "row", "col"), "rep"),
        P(("groups", "col", "row"), "rep"),
        P(),
        P(),
        P(("groups", "row"), "col", None),
    )
    out_specs = (
        P(("groups", "row"), ("col", "rep"), None),
        P(("groups", "row", "col"), "rep"),
        P(("groups", "col", "row"), "rep"),
        P("groups", None),
    )
    return jax.shard_map(
        on_device, mesh=mesh, in_specs=in_specs, out_specs=out_specs, check_vma=False
    )
```

```python
import functools

import jax
import jax.numpy as jnp
from jax import lax
from jax.experimental import pallas as pl
from jax.experimental.pallas import tpu as pltpu
from jax.sharding import PartitionSpec as P

C = 32
S = 256
LANES = 128
F32 = jnp.float32
BF16 = jnp.bfloat16
NT = (((1,), (1,)), ((), ()))


def tile_plan(left_features, right_features, weight, bias, cotangent):
    left_rows = lax.all_gather(left_features, "col", axis=0, tiled=True)
    right_rows = lax.all_gather(right_features, "row", axis=0, tiled=True)
    row_count = left_rows.shape[0]
    col_count = right_rows.shape[0]
    out_width = weight.shape[1]
    left_block = left_rows.reshape(row_count, -1, C)
    right_block = right_rows.reshape(col_count, -1, C)
    outer_sum = jnp.einsum(
        "isc,jsd->ijcd", left_block, right_block, preferred_element_type=jnp.float32
    )
    half_mean = (outer_sum / S).astype(jnp.bfloat16).reshape(row_count * col_count, C * C)
    proj_part = jnp.dot(half_mean, weight, preferred_element_type=jnp.float32).reshape(
        row_count, col_count, out_width
    )
    pair_sum = lax.psum_scatter(proj_part, "rep", scatter_dimension=1, tiled=True)
    pair_out = pair_sum + bias
    flat_grad = cotangent.reshape(row_count * col_count, out_width)
    weight_part = jnp.einsum("pk,pe->ke", half_mean, flat_grad, preferred_element_type=jnp.float32)
    weight_grad = lax.psum(weight_part, ("row", "col", "rep"))
    grad_mean = jnp.einsum("pe,ke->pk", flat_grad, weight, preferred_element_type=jnp.float32) / S
    grad_mean = grad_mean.astype(jnp.bfloat16).reshape(row_count, col_count, C, C)
    left_part = jnp.einsum(
        "ijcd,jsd->isc", grad_mean, right_block, preferred_element_type=jnp.float32
    ).reshape(row_count, -1)
    right_part = jnp.einsum(
        "ijcd,isc->jsd", grad_mean, left_block, preferred_element_type=jnp.float32
    ).reshape(col_count, -1)
    left_sum = lax.psum_scatter(left_part, "col", scatter_dimension=0, tiled=True)
    right_sum = lax.psum_scatter(right_part, "row", scatter_dimension=0, tiled=True)
    return (pair_out, left_sum.astype(jnp.bfloat16), right_sum.astype(jnp.bfloat16), weight_grad)


def exchange(x, axis, flip, size):
    return lax.ppermute(x, axis, [(k, k ^ flip) for k in range(size)])


def swap_blocks(blocks, width):
    count = len(blocks)
    lane_block = lax.broadcasted_iota(jnp.int32, blocks[0].shape, 1) // width
    bit = 1
    while bit < count:
        upper = (lane_block & bit) != 0
        out = list(blocks)
        for a in range(count):
            if a & bit == 0:
                low, high = blocks[a], blocks[a | bit]
                out[a] = jnp.where(upper, pltpu.roll(high, bit * width, 1), low)
                out[a | bit] = jnp.where(upper, high, pltpu.roll(low, LANES - bit * width, 1))
        blocks = out
        bit *= 2
    return blocks


def block_kernel(left_in, right_in, cotangent_in, block, left, right, cotangent, scratch, sems):
    pairs = ((left_in, left), (right_in, right), (cotangent_in, cotangent))
    copies = [pltpu.make_async_copy(source, into, sems.at[k]) for k, (source, into) in enumerate(pairs)]
    for copy in copies:
        copy.start()
    for copy in copies:
        copy.wait()
    held, width = left.shape
    groups = width // LANES
    for at, ref in ((0, left), (held * groups, right)):
        for g in range(groups):
            scratch[pl.ds(at + g, held, stride=groups), :] = ref[:, g * LANES:(g + 1) * LANES].astype(F32)
    turned = scratch[...].T
    rows = swap_blocks([turned[k * C:(k + 1) * C, :] for k in range(LANES // C)], C)
    block[0, :LANES, :] = jnp.concatenate(rows, axis=0).astype(BF16)
    per_row, per_col, _ = cotangent.shape
    cot = cotangent[...].astype(F32)
    parts = [cot[:, j, :] for j in range(per_col)]
    block[0, LANES:, :] = jnp.concatenate(parts, axis=0).astype(BF16)


def turn_back(rows, scratch, left_grad, right_grad):
    held, width = left_grad.shape
    groups = width // LANES
    blocks = swap_blocks([rows[k * C:(k + 1) * C, :] for k in range(LANES // C)], C)
    scratch[...] = jnp.concatenate(blocks, axis=0).T
    for at, ref in ((0, left_grad), (held * groups, right_grad)):
        for g in range(groups):
            ref[:, g * LANES:(g + 1) * LANES] = scratch[pl.ds(at + g, held, stride=groups), :].astype(BF16)


def spread(source, col, slots, first, into, stride):
    for slot in range(slots):
        for t in range(2):
            at = (col ^ slot) * 2 + t
            into[pl.ds(at, C, stride=stride), :] = source[slot, first + t * C:first + (t + 1) * C, :].astype(F32)


def spread_cot(source, col, slots, rows, into):
    per_row = 2 * slots
    for slot in range(slots):
        cot = source[slot, 4 * C:, :].astype(F32)
        for j in range(2 * rows):
            at = pl.multiple_of(((col ^ slot) * 2 + j % 2) * per_row, per_row)
            into[j // 2, pl.ds(at, per_row), :] = cot[j * per_row:(j + 1) * per_row, :]


def mixing_rows(outer_weight, cot_rows):
    tokens = cot_rows[0].shape[0]
    copies = LANES // tokens
    repeated = jnp.concatenate([jnp.concatenate([rows] * copies, axis=0) for rows in cot_rows], axis=0).astype(BF16)
    grads = lax.dot_general(outer_weight, repeated, NT, preferred_element_type=F32)
    copy_of = lax.broadcasted_iota(jnp.int32, (C, LANES), 1) // tokens
    out = []
    for two in range(2):
        lanes = grads[:, two * LANES:(two + 1) * LANES]
        parts = []
        for group in range(C // copies):
            first = group * copies * C
            part = lanes[first:first + C, :]
            for k in range(1, copies):
                at = first + k * C
                part = jnp.where(copy_of == k, lanes[at:at + C, :], part)
            parts.append((part * (1.0 / S)).astype(BF16))
        out.append(jnp.concatenate(parts, axis=1))
    return jnp.concatenate(out, axis=0)


def left_cots(cot, half, col, slots):
    per_row = 2 * slots
    return [cot[half, pl.ds(col * 2 + t, per_row, stride=per_row), :] for t in range(2)]


def right_cots(cot, half, col, slots):
    per_row = 2 * slots
    return [cot[half, pl.ds(pl.multiple_of((col * 2 + t) * per_row, per_row), per_row), :] for t in range(2)]


def near_kernel(rows, near, weight, bias, lefts, cot, grads, far_mix, weight_t, bias_out, spread_right, weight_dc):
    slots = near.shape[0]
    row, col = lax.axis_index("row"), lax.axis_index("col")
    tokens = 2 * slots
    spread(near, col, slots, 0, lefts, tokens)
    spread(near, col, slots, 2 * C, spread_right, tokens)
    spread_cot(near, col, slots, rows, cot)
    all_weight = weight[...]
    weight_dc[...] = jnp.swapaxes(all_weight.astype(F32).reshape(C, C, LANES), 0, 1).reshape(C * C, LANES).astype(BF16)
    weight_t[...] = all_weight.astype(F32).T.astype(BF16)
    bias_out[...] = bias[...]
    mix = mixing_rows(weight_dc[...], left_cots(cot, row, col, slots))
    grads[:2 * C, :] = jnp.dot(mix, spread_right[...].astype(BF16), preferred_element_type=F32)
    far_mix[...] = mixing_rows(weight_dc[...], left_cots(cot, 1 - row, col, slots))
    mix = mixing_rows(all_weight, right_cots(cot, row, col, slots))
    grads[2 * C:, :] = jnp.dot(mix, lefts[...].astype(BF16), preferred_element_type=F32)


def far_kernel(
    rows, far, near, other_near, near_lefts, near_grads, far_mix, weight,
    lefts, all_near_lefts, near_rights, cot, left_grad, right_grad, spread_right, turned,
):
    slots = far.shape[0]
    row, col, rep = lax.axis_index("row"), lax.axis_index("col"), lax.axis_index("rep")
    tokens = 2 * slots
    all_near_lefts[rep] = near_lefts[...]
    spread(other_near, col, slots, 0, all_near_lefts.at[1 - rep], tokens)
    for slot in range(slots):
        near_rights[rep, col ^ slot] = near[slot, 2 * C:4 * C, :]
        near_rights[1 - rep, col ^ slot] = other_near[slot, 2 * C:4 * C, :]
    spread(far, col, slots, 0, lefts, tokens)
    spread(far, col, slots, 2 * C, spread_right, tokens)
    spread_cot(far, col, slots, rows, cot)
    left = jnp.dot(far_mix[...], spread_right[...].astype(BF16), preferred_element_type=F32)
    mix = mixing_rows(weight[...], right_cots(cot, row, col, slots))
    right = jnp.dot(mix, lefts[...].astype(BF16), preferred_element_type=F32)
    turn_back(near_grads[...] + jnp.concatenate([left, right], axis=0), turned, left_grad, right_grad)


def outer_kernel(
    rows, near_lefts, near_rights, near_cot, far_lefts_own, far_cot, far, other, weight_t, bias, left_in, right_in,
    pair_out, left_out, right_out, weight_out, far_lefts, far_rights, pair_scratch, pair_block, weight_grad, sems,
):
    slots = far.shape[0]
    row, col, rep = lax.axis_index("row"), lax.axis_index("col"), lax.axis_index("rep")
    copies = [
        pltpu.make_async_copy(left_in, left_out, sems.at[0]),
        pltpu.make_async_copy(right_in, right_out, sems.at[1]),
    ]
    for copy in copies:
        copy.start()
    per_row, per_col = 2 * slots, 2 * rows
    tokens = rows * per_row
    far_lefts[rep] = far_lefts_own[...]
    spread(other, col, slots, 0, far_lefts.at[1 - rep], per_row)
    for slot in range(slots):
        far_rights[rep, col ^ slot] = far[slot, 2 * C:4 * C, :]
        far_rights[1 - rep, col ^ slot] = other[slot, 2 * C:4 * C, :]
    first_row = row == 0

    def ordered(near, far_part):
        return jnp.concatenate([jnp.where(first_row, near, far_part), jnp.where(first_row, far_part, near)], axis=1)

    lefts, rights = [], []
    for half in range(2):
        near = near_lefts[half].reshape(C, per_row, LANES)
        both = ordered(near, far_lefts[half].reshape(C, per_row, LANES))
        lefts.append(both.reshape(C * tokens, LANES).astype(BF16))
        rights.append(ordered(near_rights[half], far_rights[half]).reshape(tokens * C, LANES))
    left_all, right_all = jnp.concatenate(lefts, axis=1), jnp.concatenate(rights, axis=1)
    cots = []
    for q in range(slots):
        for half in range(rows):
            at = slice(q * 2 * per_row, (q + 1) * 2 * per_row)
            near = near_cot[half, at, :].reshape(2, per_row, LANES)
            cots.append(ordered(near, far_cot[half, at, :].reshape(2, per_row, LANES)).reshape(2 * tokens, LANES))
    cot_all = jnp.concatenate(cots, axis=0).astype(BF16)

    count = LANES // tokens
    pair_t = jnp.zeros((LANES, tokens * tokens), F32)
    for g in range(C // count):
        left = left_all[g * LANES:(g + 1) * LANES, :]
        outer = lax.dot_general(right_all, left, NT, preferred_element_type=F32) * (1.0 / S)
        parts = []
        for h in range(tokens // count):
            first = h * count * C
            blocks = [outer[first + k * C:first + (k + 1) * C, :] for k in range(count)]
            parts.append(jnp.concatenate(swap_blocks(blocks, tokens), axis=0).astype(BF16))
        mean = jnp.concatenate(parts, axis=1)
        at = slice(g * count * C, (g + 1) * count * C)
        weight_grad[at, :] = jnp.dot(mean, cot_all, preferred_element_type=F32)
        copy = pltpu.make_async_copy(weight_grad.at[at], weight_out.at[at], sems.at[2 + g])
        copy.start()
        copies.append(copy)
        pair_t += jnp.dot(weight_t[:, at], mean, preferred_element_type=F32)
    pair_scratch[...] = pair_t.T
    for j in range(per_col // 2):
        column = col * per_col + rep * (per_col // 2) + j
        at = pl.multiple_of(column * tokens + row * per_row, per_row)
        pair_block[:, j, :] = pair_scratch[pl.ds(at, per_row), :] + bias[...]
    copy = pltpu.make_async_copy(pair_block, pair_out, sems.at[2 + C // count])
    copy.start()
    copies.append(copy)
    for copy in copies:
        copy.wait()


def gather_plan(rows, cols, left_features, right_features, weight, bias, cotangent):
    held, width = left_features.shape
    seqs = width // C
    tokens = held * rows * cols
    half_span = tokens // rows * C
    per_row, per_col, e = cotangent.shape
    vmem = pl.BlockSpec(memory_space=pltpu.VMEM)
    anywhere = pl.BlockSpec(memory_space=pl.ANY)
    params = pltpu.CompilerParams(vmem_limit_bytes=32 * 1024 * 1024)
    array = jax.ShapeDtypeStruct

    block = pl.pallas_call(
        block_kernel,
        out_shape=array((1, 2 * held * C + per_row * per_col, seqs), BF16),
        in_specs=[pl.BlockSpec(memory_space=pltpu.HBM)] * 3,
        out_specs=vmem,
        scratch_shapes=[
            pltpu.VMEM((held, width), BF16),
            pltpu.VMEM((held, width), BF16),
            pltpu.VMEM((per_row, per_col, e), BF16),
            pltpu.VMEM((LANES, LANES), F32),
            pltpu.SemaphoreType.DMA((3,)),
        ],
        compiler_params=params,
        name="own_block",
    )(*(pltpu.with_memory_space_constraint(x, pltpu.HBM) for x in (left_features, right_features, cotangent)))
    flip = 1
    while flip < cols:
        block = jnp.concatenate([block, exchange(block, "col", flip, cols)], axis=0)
        flip *= 2
    far = exchange(block, "row", 1, rows)
    other_near = exchange(block, "rep", 1, 2)
    other_far = exchange(far, "rep", 1, 2)

    lefts = array((half_span, seqs), F32)
    cots = array((rows, cols * held * per_row, e), F32)
    near_lefts, near_cot, near_grads, far_mix, weight_t, bias_row = pl.pallas_call(
        functools.partial(near_kernel, rows),
        out_shape=(
            lefts,
            cots,
            array((2 * held * C, seqs), F32),
            array((held * C, half_span), BF16),
            array((e, C * C), BF16),
            array((1, e), F32),
        ),
        in_specs=[vmem] * 3,
        out_specs=(vmem,) * 6,
        scratch_shapes=[pltpu.VMEM((half_span, seqs), F32), pltpu.VMEM((C * C, e), BF16)],
        compiler_params=params,
        cost_estimate=pl.CostEstimate(flops=300_000_000, bytes_accessed=2_000_000, transcendentals=0),
        name="near_part",
    )(block, weight, bias.reshape(1, e))

    far_lefts, both_near_lefts, near_rights, far_cot, left_grad, right_grad = pl.pallas_call(
        functools.partial(far_kernel, rows),
        out_shape=(
            lefts,
            array((2, half_span, seqs), F32),
            array((2, cols, 2 * C, seqs), BF16),
            cots,
            array((held, width), BF16),
            array((held, width), BF16),
        ),
        in_specs=[vmem] * 7,
        out_specs=(vmem,) * 6,
        scratch_shapes=[pltpu.VMEM((half_span, seqs), F32), pltpu.VMEM((LANES, LANES), F32)],
        compiler_params=params,
        cost_estimate=pl.CostEstimate(flops=10_000_000_000, bytes_accessed=1_000_000, transcendentals=0),
        name="far_part",
    )(far, block, other_near, near_lefts, near_grads, far_mix, weight)

    return tuple(pl.pallas_call(
        functools.partial(outer_kernel, rows),
        out_shape=(
            array((per_row, per_col // 2, e), F32),
            array((held, width), BF16),
            array((held, width), BF16),
            array((C * C, e), F32),
        ),
        in_specs=[vmem] * 11,
        out_specs=(anywhere,) * 4,
        scratch_shapes=[
            pltpu.VMEM((2, half_span, seqs), F32),
            pltpu.VMEM((2, cols, 2 * C, seqs), BF16),
            pltpu.VMEM((tokens * tokens, e), F32),
            pltpu.VMEM((per_row, per_col // 2, e), F32),
            pltpu.VMEM((C * C, e), F32),
            pltpu.SemaphoreType.DMA((3 + C * tokens // LANES,)),
        ],
        compiler_params=params,
        name="outer_mean",
    )(both_near_lefts, near_rights, near_cot, far_lefts, far_cot, far, other_far, weight_t, bias_row, left_grad, right_grad))


def solution(mesh):
    rows, cols = mesh.shape["row"], mesh.shape["col"]

    def on_device(left_features, right_features, weight, bias, cotangent):
        held, width = left_features.shape
        tokens = held * rows * cols
        small = held == 2 and rows == 2 and cols & (cols - 1) == 0 and LANES % tokens == 0 and tokens == 16
        if small and width == LANES * C and weight.shape[1] == LANES and C % (LANES // tokens) == 0:
            return gather_plan(rows, cols, left_features, right_features, weight, bias, cotangent)
        return tile_plan(left_features, right_features, weight, bias, cotangent)

    in_specs = (
        P(("groups", "row", "col"), "rep"),
        P(("groups", "col", "row"), "rep"),
        P(),
        P(),
        P(("groups", "row"), "col", None),
    )
    out_specs = (
        P(("groups", "row"), ("col", "rep"), None),
        P(("groups", "row", "col"), "rep"),
        P(("groups", "col", "row"), "rep"),
        P("groups", None),
    )
    return jax.shard_map(
        on_device, mesh=mesh, in_specs=in_specs, out_specs=out_specs, check_vma=False
    )
```

```python
import functools

import jax
import jax.numpy as jnp
from jax import lax
from jax.experimental import pallas as pl
from jax.experimental.pallas import tpu as pltpu
from jax.sharding import PartitionSpec as P

C = 32
S = 256
LANES = 128
F32 = jnp.float32
BF16 = jnp.bfloat16
NT = (((1,), (1,)), ((), ()))


def tile_plan(left_features, right_features, weight, bias, cotangent):
    left_rows = lax.all_gather(left_features, "col", axis=0, tiled=True)
    right_rows = lax.all_gather(right_features, "row", axis=0, tiled=True)
    row_count = left_rows.shape[0]
    col_count = right_rows.shape[0]
    out_width = weight.shape[1]
    left_block = left_rows.reshape(row_count, -1, C)
    right_block = right_rows.reshape(col_count, -1, C)
    outer_sum = jnp.einsum(
        "isc,jsd->ijcd", left_block, right_block, preferred_element_type=jnp.float32
    )
    half_mean = (outer_sum / S).astype(jnp.bfloat16).reshape(row_count * col_count, C * C)
    proj_part = jnp.dot(half_mean, weight, preferred_element_type=jnp.float32).reshape(
        row_count, col_count, out_width
    )
    pair_sum = lax.psum_scatter(proj_part, "rep", scatter_dimension=1, tiled=True)
    pair_out = pair_sum + bias
    flat_grad = cotangent.reshape(row_count * col_count, out_width)
    weight_part = jnp.einsum("pk,pe->ke", half_mean, flat_grad, preferred_element_type=jnp.float32)
    weight_grad = lax.psum(weight_part, ("row", "col", "rep"))
    grad_mean = jnp.einsum("pe,ke->pk", flat_grad, weight, preferred_element_type=jnp.float32) / S
    grad_mean = grad_mean.astype(jnp.bfloat16).reshape(row_count, col_count, C, C)
    left_part = jnp.einsum(
        "ijcd,jsd->isc", grad_mean, right_block, preferred_element_type=jnp.float32
    ).reshape(row_count, -1)
    right_part = jnp.einsum(
        "ijcd,isc->jsd", grad_mean, left_block, preferred_element_type=jnp.float32
    ).reshape(col_count, -1)
    left_sum = lax.psum_scatter(left_part, "col", scatter_dimension=0, tiled=True)
    right_sum = lax.psum_scatter(right_part, "row", scatter_dimension=0, tiled=True)
    return (pair_out, left_sum.astype(jnp.bfloat16), right_sum.astype(jnp.bfloat16), weight_grad)


def exchange(x, axis, flip, size):
    return lax.ppermute(x, axis, [(k, k ^ flip) for k in range(size)])


def swap_blocks(blocks, width):
    count = len(blocks)
    lane_block = lax.broadcasted_iota(jnp.int32, blocks[0].shape, 1) // width
    bit = 1
    while bit < count:
        upper = (lane_block & bit) != 0
        out = list(blocks)
        for a in range(count):
            if a & bit == 0:
                low, high = blocks[a], blocks[a | bit]
                out[a] = jnp.where(upper, pltpu.roll(high, bit * width, 1), low)
                out[a | bit] = jnp.where(upper, high, pltpu.roll(low, LANES - bit * width, 1))
        blocks = out
        bit *= 2
    return blocks


def skew_blocks(blocks, width):
    count = len(blocks)
    lane_block = lax.broadcasted_iota(jnp.int32, blocks[0].shape, 1) // width
    blocks = [pltpu.roll(x, k * width, 1) if k else x for k, x in enumerate(blocks)]
    bit = 1
    while bit < count:
        upper = (lane_block & bit) != 0
        blocks = [jnp.where(upper, blocks[(m + bit) % count], blocks[m]) for m in range(count)]
        bit *= 2
    return [blocks[-c % count] for c in range(count)]


def block_kernel(left_in, right_in, cotangent_in, bias_in, block, bias, left, right, cotangent, scratch, sems):
    pairs = ((left_in, left), (right_in, right), (cotangent_in, cotangent), (bias_in, bias))
    copies = [pltpu.make_async_copy(source, into, sems.at[k]) for k, (source, into) in enumerate(pairs)]
    for copy in copies:
        copy.start()
    for copy in copies:
        copy.wait()
    held, width = left.shape
    groups = width // LANES
    for at, ref in ((0, left), (held * groups, right)):
        for g in range(groups):
            scratch[pl.ds(at + g, held, stride=groups), :] = ref[:, g * LANES:(g + 1) * LANES].astype(F32)
    turned = scratch[...].T
    rows = swap_blocks([turned[k * C:(k + 1) * C, :] for k in range(LANES // C)], C)
    block[0, :LANES, :] = jnp.concatenate(rows, axis=0).astype(BF16)
    per_row, per_col, _ = cotangent.shape
    cot = cotangent[...].astype(F32)
    parts = [cot[:, j, :] for j in range(per_col)]
    block[0, LANES:, :] = jnp.concatenate(parts, axis=0).astype(BF16)


def turn_back(rows, scratch, left_grad, right_grad):
    held, width = left_grad.shape
    groups = width // LANES
    blocks = swap_blocks([rows[k * C:(k + 1) * C, :] for k in range(LANES // C)], C)
    scratch[...] = jnp.concatenate(blocks, axis=0).T
    for at, ref in ((0, left_grad), (held * groups, right_grad)):
        for g in range(groups):
            ref[:, g * LANES:(g + 1) * LANES] = scratch[pl.ds(at + g, held, stride=groups), :].astype(BF16)


def spread(source, col, slots, first, into, stride):
    for slot in range(slots):
        for t in range(2):
            at = (col ^ slot) * 2 + t
            into[pl.ds(at, C, stride=stride), :] = source[slot, first + t * C:first + (t + 1) * C, :].astype(F32)


def spread_cot(source, col, slots, rows, into):
    per_row = 2 * slots
    for slot in range(slots):
        cot = source[slot, 4 * C:, :].astype(F32)
        for j in range(2 * rows):
            at = pl.multiple_of(((col ^ slot) * 2 + j % 2) * per_row, per_row)
            into[j // 2, pl.ds(at, per_row), :] = cot[j * per_row:(j + 1) * per_row, :]


def mixing_rows(outer_weight, cot_rows):
    tokens = cot_rows[0].shape[0]
    copies = LANES // tokens
    repeated = jnp.concatenate([jnp.concatenate([rows] * copies, axis=0) for rows in cot_rows], axis=0).astype(BF16)
    grads = lax.dot_general(outer_weight, repeated, NT, preferred_element_type=F32)
    copy_of = lax.broadcasted_iota(jnp.int32, (C, LANES), 1) // tokens
    out = []
    for two in range(2):
        lanes = grads[:, two * LANES:(two + 1) * LANES]
        parts = []
        for group in range(C // copies):
            first = group * copies * C
            part = lanes[first:first + C, :]
            for k in range(1, copies):
                at = first + k * C
                part = jnp.where(copy_of == k, lanes[at:at + C, :], part)
            parts.append((part * (1.0 / S)).astype(BF16))
        out.append(jnp.concatenate(parts, axis=1))
    return jnp.concatenate(out, axis=0)


def left_cots(cot, half, col, slots):
    per_row = 2 * slots
    return [cot[half, pl.ds(col * 2 + t, per_row, stride=per_row), :] for t in range(2)]


def right_cots(cot, half, col, slots):
    per_row = 2 * slots
    return [cot[half, pl.ds(pl.multiple_of((col * 2 + t) * per_row, per_row), per_row), :] for t in range(2)]


def near_kernel(rows, near, weight, lefts, cot, grads, far_mix, spread_right, weight_dc):
    slots = near.shape[0]
    row, col = lax.axis_index("row"), lax.axis_index("col")
    tokens = 2 * slots
    spread(near, col, slots, 0, lefts, tokens)
    spread(near, col, slots, 2 * C, spread_right, tokens)
    spread_cot(near, col, slots, rows, cot)
    all_weight = weight[...]
    weight_dc[...] = jnp.swapaxes(all_weight.astype(F32).reshape(C, C, LANES), 0, 1).reshape(C * C, LANES).astype(BF16)
    mix = mixing_rows(weight_dc[...], left_cots(cot, row, col, slots))
    grads[:2 * C, :] = jnp.dot(mix, spread_right[...].astype(BF16), preferred_element_type=F32)
    far_mix[...] = mixing_rows(weight_dc[...], left_cots(cot, 1 - row, col, slots))
    mix = mixing_rows(all_weight, right_cots(cot, row, col, slots))
    grads[2 * C:, :] = jnp.dot(mix, lefts[...].astype(BF16), preferred_element_type=F32)


def ordered(first, near, far):
    return jnp.concatenate([jnp.where(first, near, far), jnp.where(first, far, near)], axis=1)


def far_kernel(
    rows, far, near, near_lefts, near_cot, near_grads, far_mix, weight,
    lefts, rights, cot_all, left_grad, right_grad, far_lefts, far_cot, spread_right, turned,
):
    slots = far.shape[0]
    row, col = lax.axis_index("row"), lax.axis_index("col")
    per_row = 2 * slots
    tokens = rows * per_row
    spread(far, col, slots, 0, far_lefts, per_row)
    spread(far, col, slots, 2 * C, spread_right, per_row)
    spread_cot(far, col, slots, rows, far_cot)
    left = jnp.dot(far_mix[...], spread_right[...].astype(BF16), preferred_element_type=F32)
    mix = mixing_rows(weight[...], right_cots(far_cot, row, col, slots))
    right = jnp.dot(mix, far_lefts[...].astype(BF16), preferred_element_type=F32)
    turn_back(near_grads[...] + jnp.concatenate([left, right], axis=0), turned, left_grad, right_grad)
    first = row == 0
    both = ordered(first, near_lefts[...].reshape(C, per_row, LANES), far_lefts[...].reshape(C, per_row, LANES))
    lefts[...] = both.reshape(C * tokens, LANES).astype(BF16)
    sort_rights(near, far, row, col, slots, rows, 2 * C, rights)
    for q in range(slots):
        at = slice(q * 2 * per_row, (q + 1) * 2 * per_row)
        for half in range(rows):
            near_rows = near_cot[half, at, :].reshape(2, per_row, LANES)
            both = ordered(first, near_rows, far_cot[half, at, :].reshape(2, per_row, LANES))
            first_row = (q * rows + half) * 2 * tokens
            cot_all[first_row:first_row + 2 * tokens, :] = both.reshape(2 * tokens, LANES).astype(BF16)


def sort_rights(near, far, row, col, slots, rows, first, into):
    for half, source in enumerate((near, far)):
        for slot in range(slots):
            chip = (col ^ slot) * rows + lax.rem(row + half, rows)
            into[pl.ds(pl.multiple_of(chip * 2 * C, 2 * C), 2 * C), :] = source[slot, first:first + 2 * C, :]


def outer_kernel(
    rows, own_lefts, own_rights, other, cot_all, weight, bias, left_in, right_in,
    pair_out, left_out, right_out, weight_out, spread_left, lefts, rights, pair_block, weight_grad, sems,
):
    slots = other.shape[0] // rows
    row, col, rep = lax.axis_index("row"), lax.axis_index("col"), lax.axis_index("rep")
    copies = [
        pltpu.make_async_copy(left_in, left_out, sems.at[0]),
        pltpu.make_async_copy(right_in, right_out, sems.at[1]),
    ]
    for copy in copies:
        copy.start()
    per_row, per_col = 2 * slots, 2 * rows
    tokens = rows * per_row
    for half in range(rows):
        first = lax.rem(row + half, rows) * per_row
        for slot in range(slots):
            for t in range(2):
                at = first + (col ^ slot) * 2 + t
                block = other[half * slots + slot, t * C:(t + 1) * C, :]
                spread_left[pl.ds(at, C, stride=tokens), :] = block.astype(F32)
    lefts[rep] = own_lefts[...]
    lefts[1 - rep] = spread_left[...].astype(BF16)
    rights[rep] = own_rights[...]
    sort_rights(other.at[:slots], other.at[slots:], row, col, slots, rows, 2 * C, rights.at[1 - rep])

    def all_of(ref, at):
        return jnp.concatenate([ref[0, at, :], ref[1, at, :]], axis=1)

    right_all = all_of(rights, slice(None))
    count = LANES // tokens
    groups = C // count
    means = [[[] for _ in range(groups)] for _ in range(count)]
    for g in range(groups):
        left = all_of(lefts, slice(g * LANES, (g + 1) * LANES))
        outer = lax.dot_general(right_all, left, NT, preferred_element_type=F32) * (1.0 / S)
        for h in range(tokens // count):
            first = h * count * C
            blocks = [outer[first + k * C:first + (k + 1) * C, :] for k in range(count)]
            for c, mean in enumerate(skew_blocks(blocks, tokens)):
                means[c][g].append(mean)
    for c in range(count):
        mean = jnp.concatenate([jnp.concatenate(halves, axis=1) for halves in means[c]], axis=0).astype(BF16)
        cot = jnp.concatenate(
            [
                cot_all[at:at + tokens, :]
                for h in range(tokens // count)
                for at in [(h * count + (k - c) % count) * tokens for k in range(count)]
            ],
            axis=0,
        )
        part = jnp.dot(mean, cot, preferred_element_type=F32)
        at = slice(c * C, (c + 1) * C)
        weight_grad[:, at, :] = part.reshape(groups, C, LANES)
        copy = pltpu.make_async_copy(weight_grad.at[:, at], weight_out.at[:, at], sems.at[3 + c])
        copy.start()
        copies.append(copy)

    own_count = per_col // 2
    at = pl.ds(pl.multiple_of((col * per_col + rep * own_count) * C, own_count * C), own_count * C)
    own = lax.dot_general(all_of(lefts, slice(None)), all_of(rights, at), NT, preferred_element_type=F32) * (1.0 / S)
    own_mean = jnp.concatenate(
        [
            jnp.concatenate([own[c * tokens:(c + 1) * tokens, t * C:(t + 1) * C] for c in range(C)], axis=1)
            for t in range(own_count)
        ],
        axis=0,
    ).astype(BF16)
    own_pairs = jnp.dot(own_mean, weight[...], preferred_element_type=F32) + bias[...]
    for t in range(own_count):
        lower = own_pairs[t * tokens:t * tokens + per_row, :]
        pair_block[:, t, :] = jnp.where(row == 0, lower, own_pairs[t * tokens + per_row:(t + 1) * tokens, :])
    copy = pltpu.make_async_copy(pair_block, pair_out, sems.at[2])
    copy.start()
    copies.append(copy)
    for copy in copies:
        copy.wait()


def gather_plan(rows, cols, left_features, right_features, weight, bias, cotangent):
    held, width = left_features.shape
    seqs = width // C
    tokens = held * rows * cols
    half_span = tokens // rows * C
    per_row, per_col, e = cotangent.shape
    vmem = pl.BlockSpec(memory_space=pltpu.VMEM)
    anywhere = pl.BlockSpec(memory_space=pl.ANY)
    params = pltpu.CompilerParams(vmem_limit_bytes=32 * 1024 * 1024)
    array = jax.ShapeDtypeStruct

    in_hbm = [left_features, right_features, cotangent, bias.reshape(1, e)]
    block, bias_row = pl.pallas_call(
        block_kernel,
        out_shape=(array((1, 2 * held * C + per_row * per_col, seqs), BF16), array((1, e), F32)),
        in_specs=[pl.BlockSpec(memory_space=pltpu.HBM)] * 4,
        out_specs=(vmem, vmem),
        scratch_shapes=[
            pltpu.VMEM((held, width), BF16),
            pltpu.VMEM((held, width), BF16),
            pltpu.VMEM((per_row, per_col, e), BF16),
            pltpu.VMEM((LANES, LANES), F32),
            pltpu.SemaphoreType.DMA((4,)),
        ],
        compiler_params=params,
        name="own_block",
    )(*(pltpu.with_memory_space_constraint(x, pltpu.HBM) for x in in_hbm))
    flip = 1
    while flip < cols:
        arrived = exchange(block, "col", flip, cols)
        if flip * 2 == cols:
            far = [exchange(block, "row", 1, rows), exchange(arrived, "row", 1, rows)]
        block = jnp.concatenate([block, arrived], axis=0)
        flip *= 2
    far = jnp.concatenate(far, axis=0)
    other = exchange(jnp.concatenate([block, far], axis=0), "rep", 1, 2)

    lefts = array((half_span, seqs), F32)
    cots = array((rows, cols * held * per_row, e), F32)
    near_lefts, near_cot, near_grads, far_mix = pl.pallas_call(
        functools.partial(near_kernel, rows),
        out_shape=(
            lefts,
            cots,
            array((2 * held * C, seqs), F32),
            array((held * C, half_span), BF16),
        ),
        in_specs=[vmem] * 2,
        out_specs=(vmem,) * 4,
        scratch_shapes=[pltpu.VMEM((half_span, seqs), F32), pltpu.VMEM((C * C, e), BF16)],
        compiler_params=params,
        cost_estimate=pl.CostEstimate(flops=300_000_000, bytes_accessed=2_000_000, transcendentals=0),
        name="near_part",
    )(block, weight)

    own_lefts, own_rights, cot_all, left_grad, right_grad = pl.pallas_call(
        functools.partial(far_kernel, rows),
        out_shape=(
            array((tokens * C, seqs), BF16),
            array((tokens * C, seqs), BF16),
            array((tokens * tokens, e), BF16),
            array((held, width), BF16),
            array((held, width), BF16),
        ),
        in_specs=[vmem] * 7,
        out_specs=(vmem,) * 5,
        scratch_shapes=[
            pltpu.VMEM((half_span, seqs), F32),
            pltpu.VMEM(cots.shape, F32),
            pltpu.VMEM((half_span, seqs), F32),
            pltpu.VMEM((LANES, LANES), F32),
        ],
        compiler_params=params,
        cost_estimate=pl.CostEstimate(flops=10_000_000_000, bytes_accessed=1_000_000, transcendentals=0),
        name="far_part",
    )(far, block, near_lefts, near_cot, near_grads, far_mix, weight)

    split = (C * tokens // LANES, LANES // tokens * C, e)
    pair_out, left_grad, right_grad, weight_grad = pl.pallas_call(
        functools.partial(outer_kernel, rows),
        out_shape=(
            array((per_row, per_col // 2, e), F32),
            array((held, width), BF16),
            array((held, width), BF16),
            array(split, F32),
        ),
        in_specs=[vmem] * 8,
        out_specs=(anywhere,) * 4,
        scratch_shapes=[
            pltpu.VMEM((tokens * C, seqs), F32),
            pltpu.VMEM((2, tokens * C, seqs), BF16),
            pltpu.VMEM((2, tokens * C, seqs), BF16),
            pltpu.VMEM((per_row, per_col // 2, e), F32),
            pltpu.VMEM(split, F32),
            pltpu.SemaphoreType.DMA((3 + LANES // tokens,)),
        ],
        compiler_params=params,
        name="outer_mean",
    )(own_lefts, own_rights, other, cot_all, weight, bias_row, left_grad, right_grad)
    return pair_out, left_grad, right_grad, weight_grad.reshape(C * C, e)


def solution(mesh):
    rows, cols = mesh.shape["row"], mesh.shape["col"]

    def on_device(left_features, right_features, weight, bias, cotangent):
        held, width = left_features.shape
        tokens = held * rows * cols
        small = held == 2 and rows == 2 and cols & (cols - 1) == 0 and LANES % tokens == 0 and tokens == 16
        if small and width == LANES * C and weight.shape[1] == LANES and C % (LANES // tokens) == 0:
            return gather_plan(rows, cols, left_features, right_features, weight, bias, cotangent)
        return tile_plan(left_features, right_features, weight, bias, cotangent)

    in_specs = (
        P(("groups", "row", "col"), "rep"),
        P(("groups", "col", "row"), "rep"),
        P(),
        P(),
        P(("groups", "row"), "col", None),
    )
    out_specs = (
        P(("groups", "row"), ("col", "rep"), None),
        P(("groups", "row", "col"), "rep"),
        P(("groups", "col", "row"), "rep"),
        P("groups", None),
    )
    return jax.shard_map(
        on_device, mesh=mesh, in_specs=in_specs, out_specs=out_specs, check_vma=False
    )
```

```python
import functools

import jax
import jax.numpy as jnp
from jax import lax
from jax.experimental import pallas as pl
from jax.experimental.pallas import tpu as pltpu
from jax.sharding import PartitionSpec as P

C = 32
S = 256
LANES = 128
F32 = jnp.float32
BF16 = jnp.bfloat16
NT = (((1,), (1,)), ((), ()))


def tile_plan(left_features, right_features, weight, bias, cotangent):
    left_rows = lax.all_gather(left_features, "col", axis=0, tiled=True)
    right_rows = lax.all_gather(right_features, "row", axis=0, tiled=True)
    row_count = left_rows.shape[0]
    col_count = right_rows.shape[0]
    out_width = weight.shape[1]
    left_block = left_rows.reshape(row_count, -1, C)
    right_block = right_rows.reshape(col_count, -1, C)
    outer_sum = jnp.einsum(
        "isc,jsd->ijcd", left_block, right_block, preferred_element_type=jnp.float32
    )
    half_mean = (outer_sum / S).astype(jnp.bfloat16).reshape(row_count * col_count, C * C)
    proj_part = jnp.dot(half_mean, weight, preferred_element_type=jnp.float32).reshape(
        row_count, col_count, out_width
    )
    pair_sum = lax.psum_scatter(proj_part, "rep", scatter_dimension=1, tiled=True)
    pair_out = pair_sum + bias
    flat_grad = cotangent.reshape(row_count * col_count, out_width)
    weight_part = jnp.einsum("pk,pe->ke", half_mean, flat_grad, preferred_element_type=jnp.float32)
    weight_grad = lax.psum(weight_part, ("row", "col", "rep"))
    grad_mean = jnp.einsum("pe,ke->pk", flat_grad, weight, preferred_element_type=jnp.float32) / S
    grad_mean = grad_mean.astype(jnp.bfloat16).reshape(row_count, col_count, C, C)
    left_part = jnp.einsum(
        "ijcd,jsd->isc", grad_mean, right_block, preferred_element_type=jnp.float32
    ).reshape(row_count, -1)
    right_part = jnp.einsum(
        "ijcd,isc->jsd", grad_mean, left_block, preferred_element_type=jnp.float32
    ).reshape(col_count, -1)
    left_sum = lax.psum_scatter(left_part, "col", scatter_dimension=0, tiled=True)
    right_sum = lax.psum_scatter(right_part, "row", scatter_dimension=0, tiled=True)
    return (pair_out, left_sum.astype(jnp.bfloat16), right_sum.astype(jnp.bfloat16), weight_grad)


def exchange(x, axis, flip, size):
    return lax.ppermute(x, axis, [(k, k ^ flip) for k in range(size)])


def swap_blocks(blocks, width):
    count = len(blocks)
    lane_block = lax.broadcasted_iota(jnp.int32, blocks[0].shape, 1) // width
    bit = 1
    while bit < count:
        upper = (lane_block & bit) != 0
        out = list(blocks)
        for a in range(count):
            if a & bit == 0:
                low, high = blocks[a], blocks[a | bit]
                out[a] = jnp.where(upper, pltpu.roll(high, bit * width, 1), low)
                out[a | bit] = jnp.where(upper, high, pltpu.roll(low, LANES - bit * width, 1))
        blocks = out
        bit *= 2
    return blocks


def skew_blocks(blocks, width):
    count = len(blocks)
    lane_block = lax.broadcasted_iota(jnp.int32, blocks[0].shape, 1) // width
    blocks = [pltpu.roll(x, k * width, 1) if k else x for k, x in enumerate(blocks)]
    bit = 1
    while bit < count:
        upper = (lane_block & bit) != 0
        blocks = [jnp.where(upper, blocks[(m + bit) % count], blocks[m]) for m in range(count)]
        bit *= 2
    return [blocks[-c % count] for c in range(count)]


def block_kernel(left_in, right_in, cotangent_in, bias_in, block, bias, left, right, cotangent, scratch, sems):
    pairs = ((left_in, left), (right_in, right), (cotangent_in, cotangent), (bias_in, bias))
    copies = [pltpu.make_async_copy(source, into, sems.at[k]) for k, (source, into) in enumerate(pairs)]
    for copy in copies:
        copy.start()
    for copy in copies:
        copy.wait()
    held, width = left.shape
    groups = width // LANES
    scratch[...] = jnp.concatenate([ref[...].astype(F32).reshape(held * groups, LANES) for ref in (left, right)], axis=0)
    turned = scratch[...].T
    rows = swap_blocks([turned[k * C:(k + 1) * C, :] for k in range(LANES // C)], C)
    block[0, :LANES, :] = jnp.concatenate(rows, axis=0).astype(BF16)
    per_row, per_col, _ = cotangent.shape
    cot = cotangent[...].astype(F32)
    parts = [cot[:, j, :] for j in range(per_col)]
    block[0, LANES:, :] = jnp.concatenate(parts, axis=0).astype(BF16)


def turn_back(rows, scratch, left_grad, right_grad):
    held, width = left_grad.shape
    groups = width // LANES
    blocks = swap_blocks([rows[k * C:(k + 1) * C, :] for k in range(LANES // C)], C)
    scratch[...] = jnp.concatenate(blocks, axis=0).T
    for at, ref in ((0, left_grad), (held * groups, right_grad)):
        for g in range(groups):
            ref[:, g * LANES:(g + 1) * LANES] = scratch[pl.ds(at + g, held, stride=groups), :].astype(BF16)


def spread(source, col, slots, first, into, stride):
    for slot in range(slots):
        for t in range(2):
            at = (col ^ slot) * 2 + t
            into[pl.ds(at, C, stride=stride), :] = source[slot, first + t * C:first + (t + 1) * C, :].astype(F32)


def spread_cot(source, col, slots, rows, into):
    per_row = 2 * slots
    for slot in range(slots):
        cot = source[slot, 4 * C:, :].astype(F32)
        for j in range(2 * rows):
            at = pl.multiple_of(((col ^ slot) * 2 + j % 2) * per_row, per_row)
            into[j // 2, pl.ds(at, per_row), :] = cot[j * per_row:(j + 1) * per_row, :]


def mixing_rows(outer_weight, cot_rows):
    tokens = cot_rows[0].shape[0]
    copies = LANES // tokens
    repeated = jnp.concatenate([jnp.concatenate([rows] * copies, axis=0) for rows in cot_rows], axis=0).astype(BF16)
    grads = lax.dot_general(outer_weight, repeated, NT, preferred_element_type=F32)
    copy_of = lax.broadcasted_iota(jnp.int32, (C, LANES), 1) // tokens
    out = []
    for two in range(2):
        lanes = grads[:, two * LANES:(two + 1) * LANES]
        parts = []
        for group in range(C // copies):
            first = group * copies * C
            part = lanes[first:first + C, :]
            for k in range(1, copies):
                at = first + k * C
                part = jnp.where(copy_of == k, lanes[at:at + C, :], part)
            parts.append((part * (1.0 / S)).astype(BF16))
        out.append(jnp.concatenate(parts, axis=1))
    return jnp.concatenate(out, axis=0)


def left_cots(cot, half, col, slots):
    per_row = 2 * slots
    return [cot[half, pl.ds(col * 2 + t, per_row, stride=per_row), :] for t in range(2)]


def right_cots(cot, half, col, slots):
    per_row = 2 * slots
    return [cot[half, pl.ds(pl.multiple_of((col * 2 + t) * per_row, per_row), per_row), :] for t in range(2)]


def near_kernel(rows, near, weight, sent, lefts, cot, grads, far_mix, spread_right, weight_dc):
    slots = near.shape[0]
    row, col = lax.axis_index("row"), lax.axis_index("col")
    tokens = 2 * slots
    spread(near, col, slots, 0, lefts, tokens)
    spread(near, col, slots, 2 * C, spread_right, tokens)
    spread_cot(near, col, slots, rows, cot)
    span = tokens * C
    sent[:span, :] = lefts[...].astype(BF16)
    for slot in range(slots):
        sent[pl.ds(pl.multiple_of(span + (col ^ slot) * 2 * C, 2 * C), 2 * C), :] = near[slot, 2 * C:4 * C, :]
    all_weight = weight[...]
    weight_dc[...] = jnp.swapaxes(all_weight.astype(F32).reshape(C, C, LANES), 0, 1).reshape(C * C, LANES).astype(BF16)
    mix = mixing_rows(weight_dc[...], left_cots(cot, row, col, slots))
    grads[:2 * C, :] = jnp.dot(mix, spread_right[...].astype(BF16), preferred_element_type=F32)
    far_mix[...] = mixing_rows(weight_dc[...], left_cots(cot, 1 - row, col, slots))
    mix = mixing_rows(all_weight, right_cots(cot, row, col, slots))
    grads[2 * C:, :] = jnp.dot(mix, lefts[...].astype(BF16), preferred_element_type=F32)


def ordered(first, near, far):
    return jnp.concatenate([jnp.where(first, near, far), jnp.where(first, far, near)], axis=1)


def far_kernel(
    rows, far, near, near_lefts, near_cot, near_grads, far_mix, weight,
    lefts, rights, cot_all, left_grad, right_grad, far_lefts, far_cot, spread_right, turned,
):
    slots = far.shape[0]
    row, col = lax.axis_index("row"), lax.axis_index("col")
    per_row = 2 * slots
    tokens = rows * per_row
    spread(far, col, slots, 0, far_lefts, per_row)
    spread(far, col, slots, 2 * C, spread_right, per_row)
    spread_cot(far, col, slots, rows, far_cot)
    left = jnp.dot(far_mix[...], spread_right[...].astype(BF16), preferred_element_type=F32)
    mix = mixing_rows(weight[...], right_cots(far_cot, row, col, slots))
    right = jnp.dot(mix, far_lefts[...].astype(BF16), preferred_element_type=F32)
    turn_back(near_grads[...] + jnp.concatenate([left, right], axis=0), turned, left_grad, right_grad)
    first = row == 0
    both = ordered(first, near_lefts[...].reshape(C, per_row, LANES), far_lefts[...].reshape(C, per_row, LANES))
    lefts[...] = both.reshape(C * tokens, LANES).astype(BF16)
    sort_rights(near, far, row, col, slots, rows, 2 * C, rights)
    for q in range(slots):
        at = slice(q * 2 * per_row, (q + 1) * 2 * per_row)
        for half in range(rows):
            near_rows = near_cot[half, at, :].reshape(2, per_row, LANES)
            both = ordered(first, near_rows, far_cot[half, at, :].reshape(2, per_row, LANES))
            first_row = (q * rows + half) * 2 * tokens
            cot_all[first_row:first_row + 2 * tokens, :] = both.reshape(2 * tokens, LANES).astype(BF16)


def sort_rights(near, far, row, col, slots, rows, first, into):
    for half, source in enumerate((near, far)):
        for slot in range(slots):
            chip = (col ^ slot) * rows + lax.rem(row + half, rows)
            into[pl.ds(pl.multiple_of(chip * 2 * C, 2 * C), 2 * C), :] = source[slot, first:first + 2 * C, :]


def outer_kernel(
    rows, slots, own_lefts, own_rights, other, cot_all, weight, bias, left_in, right_in,
    pair_out, left_out, right_out, weight_out, spread_left, lefts, rights, pair_block, weight_grad, sems,
):
    row, col, rep = lax.axis_index("row"), lax.axis_index("col"), lax.axis_index("rep")
    copies = [
        pltpu.make_async_copy(left_in, left_out, sems.at[0]),
        pltpu.make_async_copy(right_in, right_out, sems.at[1]),
    ]
    for copy in copies:
        copy.start()
    per_row, per_col = 2 * slots, 2 * rows
    tokens = rows * per_row
    span = per_row * C
    stride = (other.shape[0] - 2 * span) // slots
    for slot in range(slots):
        for t in range(2):
            at = 2 * span + slot * stride + t * C
            spread_left[pl.ds((col ^ slot) * 2 + t, C, stride=per_row), :] = other[at:at + C, :].astype(F32)
    near = other[:span, :].astype(F32).reshape(C, per_row, LANES)
    both = ordered(row == 0, near, spread_left[...].reshape(C, per_row, LANES))
    lefts[rep] = own_lefts[...]
    lefts[1 - rep] = both.reshape(C * tokens, LANES).astype(BF16)
    rights[rep] = own_rights[...]
    for q in range(slots):
        at = pl.multiple_of((q * rows + row) * 2 * C, 2 * C)
        rights[1 - rep, pl.ds(at, 2 * C), :] = other[span + q * 2 * C:span + (q + 1) * 2 * C, :]
        at = pl.multiple_of(((col ^ q) * rows + 1 - row) * 2 * C, 2 * C)
        rights[1 - rep, pl.ds(at, 2 * C), :] = other[2 * span + q * stride + 2 * C:2 * span + q * stride + 4 * C, :]

    def all_of(ref, at):
        return jnp.concatenate([ref[0, at, :], ref[1, at, :]], axis=1)

    right_all = all_of(rights, slice(None))
    count = LANES // tokens
    groups = C // count
    means = [[[] for _ in range(groups)] for _ in range(count)]
    for g in range(groups):
        if g % 2 == 0:
            left = all_of(lefts, slice(g * LANES, (g + 2) * LANES))
            wide = lax.dot_general(right_all, left, NT, preferred_element_type=F32) * (1.0 / S)
        outer = wide[:, g % 2 * LANES:(g % 2 + 1) * LANES]
        for h in range(tokens // count):
            first = h * count * C
            blocks = [outer[first + k * C:first + (k + 1) * C, :] for k in range(count)]
            for c, mean in enumerate(skew_blocks(blocks, tokens)):
                means[c][g].append(mean)
    own_count = per_col // 2
    at = pl.ds(pl.multiple_of((col * per_col + rep * own_count) * C, own_count * C), own_count * C)
    own = lax.dot_general(all_of(lefts, slice(None)), all_of(rights, at), NT, preferred_element_type=F32) * (1.0 / S)
    own_mean = jnp.concatenate(
        [
            jnp.concatenate([own[c * tokens:(c + 1) * tokens, t * C:(t + 1) * C] for c in range(C)], axis=1)
            for t in range(own_count)
        ],
        axis=0,
    ).astype(BF16)
    own_pairs = jnp.dot(own_mean, weight[...], preferred_element_type=F32) + bias[...]
    for t in range(own_count):
        lower = own_pairs[t * tokens:t * tokens + per_row, :]
        pair_block[:, t, :] = jnp.where(row == 0, lower, own_pairs[t * tokens + per_row:(t + 1) * tokens, :])
    copy = pltpu.make_async_copy(pair_block, pair_out, sems.at[2])
    copy.start()
    copies.append(copy)
    for c in range(count):
        mean = jnp.concatenate([jnp.concatenate(halves, axis=1) for halves in means[c]], axis=0).astype(BF16)
        cot = jnp.concatenate(
            [
                cot_all[at:at + tokens, :]
                for h in range(tokens // count)
                for at in [(h * count + (k - c) % count) * tokens for k in range(count)]
            ],
            axis=0,
        )
        part = jnp.dot(mean, cot, preferred_element_type=F32)
        at = slice(c * C, (c + 1) * C)
        weight_grad[:, at, :] = part.reshape(groups, C, LANES)
        copy = pltpu.make_async_copy(weight_grad.at[:, at], weight_out.at[:, at], sems.at[3 + c])
        copy.start()
        copies.append(copy)

    for copy in copies:
        copy.wait()


def gather_plan(rows, cols, left_features, right_features, weight, bias, cotangent):
    held, width = left_features.shape
    seqs = width // C
    tokens = held * rows * cols
    half_span = tokens // rows * C
    per_row, per_col, e = cotangent.shape
    vmem = pl.BlockSpec(memory_space=pltpu.VMEM)
    anywhere = pl.BlockSpec(memory_space=pl.ANY)
    params = pltpu.CompilerParams(vmem_limit_bytes=32 * 1024 * 1024)
    array = jax.ShapeDtypeStruct

    in_hbm = [left_features, right_features, cotangent, bias.reshape(1, e)]
    block, bias_row = pl.pallas_call(
        block_kernel,
        out_shape=(array((1, 2 * held * C + per_row * per_col, seqs), BF16), array((1, e), F32)),
        in_specs=[pl.BlockSpec(memory_space=pltpu.HBM)] * 4,
        out_specs=(vmem, vmem),
        scratch_shapes=[
            pltpu.VMEM((held, width), BF16),
            pltpu.VMEM((held, width), BF16),
            pltpu.VMEM((per_row, per_col, e), BF16),
            pltpu.VMEM((LANES, LANES), F32),
            pltpu.SemaphoreType.DMA((4,)),
        ],
        compiler_params=params,
        name="own_block",
    )(*(pltpu.with_memory_space_constraint(x, pltpu.HBM) for x in in_hbm))
    flip = 1
    while flip < cols:
        arrived = exchange(block, "col", flip, cols)
        if flip * 2 == cols:
            far = [exchange(block, "row", 1, rows), exchange(arrived, "row", 1, rows)]
        block = jnp.concatenate([block, arrived], axis=0)
        flip *= 2
    far = jnp.concatenate(far, axis=0)

    lefts = array((half_span, seqs), F32)
    cots = array((rows, cols * held * per_row, e), F32)
    near_sent, near_lefts, near_cot, near_grads, far_mix = pl.pallas_call(
        functools.partial(near_kernel, rows),
        out_shape=(
            array((2 * half_span, seqs), BF16),
            lefts,
            cots,
            array((2 * held * C, seqs), F32),
            array((held * C, half_span), BF16),
        ),
        in_specs=[vmem] * 2,
        out_specs=(vmem,) * 5,
        scratch_shapes=[pltpu.VMEM((half_span, seqs), F32), pltpu.VMEM((C * C, e), BF16)],
        compiler_params=params,
        cost_estimate=pl.CostEstimate(flops=300_000_000, bytes_accessed=2_000_000, transcendentals=0),
        name="near_part",
    )(block, weight)
    other = exchange(jnp.concatenate([near_sent, far.reshape(-1, seqs)], axis=0), "rep", 1, 2)

    own_lefts, own_rights, cot_all, left_grad, right_grad = pl.pallas_call(
        functools.partial(far_kernel, rows),
        out_shape=(
            array((tokens * C, seqs), BF16),
            array((tokens * C, seqs), BF16),
            array((tokens * tokens, e), BF16),
            array((held, width), BF16),
            array((held, width), BF16),
        ),
        in_specs=[vmem] * 7,
        out_specs=(vmem,) * 5,
        scratch_shapes=[
            pltpu.VMEM((half_span, seqs), F32),
            pltpu.VMEM(cots.shape, F32),
            pltpu.VMEM((half_span, seqs), F32),
            pltpu.VMEM((LANES, LANES), F32),
        ],
        compiler_params=params,
        cost_estimate=pl.CostEstimate(flops=10_000_000_000, bytes_accessed=1_000_000, transcendentals=0),
        name="far_part",
    )(far, block, near_lefts, near_cot, near_grads, far_mix, weight)

    split = (C * tokens // LANES, LANES // tokens * C, e)
    pair_out, left_grad, right_grad, weight_grad = pl.pallas_call(
        functools.partial(outer_kernel, rows, cols),
        out_shape=(
            array((per_row, per_col // 2, e), F32),
            array((held, width), BF16),
            array((held, width), BF16),
            array(split, F32),
        ),
        in_specs=[vmem] * 8,
        out_specs=(anywhere,) * 4,
        scratch_shapes=[
            pltpu.VMEM((half_span, seqs), F32),
            pltpu.VMEM((2, tokens * C, seqs), BF16),
            pltpu.VMEM((2, tokens * C, seqs), BF16),
            pltpu.VMEM((per_row, per_col // 2, e), F32),
            pltpu.VMEM(split, F32),
            pltpu.SemaphoreType.DMA((3 + LANES // tokens,)),
        ],
        compiler_params=params,
        name="outer_mean",
    )(own_lefts, own_rights, other, cot_all, weight, bias_row, left_grad, right_grad)
    return pair_out, left_grad, right_grad, weight_grad.reshape(C * C, e)


def solution(mesh):
    rows, cols = mesh.shape["row"], mesh.shape["col"]

    def on_device(left_features, right_features, weight, bias, cotangent):
        held, width = left_features.shape
        tokens = held * rows * cols
        small = held == 2 and rows == 2 and cols & (cols - 1) == 0 and LANES % tokens == 0 and tokens == 16
        if small and width == LANES * C and weight.shape[1] == LANES and C % (LANES // tokens) == 0:
            return gather_plan(rows, cols, left_features, right_features, weight, bias, cotangent)
        return tile_plan(left_features, right_features, weight, bias, cotangent)

    in_specs = (
        P(("groups", "row", "col"), "rep"),
        P(("groups", "col", "row"), "rep"),
        P(),
        P(),
        P(("groups", "row"), "col", None),
    )
    out_specs = (
        P(("groups", "row"), ("col", "rep"), None),
        P(("groups", "row", "col"), "rep"),
        P(("groups", "col", "row"), "rep"),
        P("groups", None),
    )
    return jax.shard_map(
        on_device, mesh=mesh, in_specs=in_specs, out_specs=out_specs, check_vma=False
    )
```

```python
import functools

import jax
import jax.numpy as jnp
from jax import lax
from jax.experimental import pallas as pl
from jax.experimental.pallas import tpu as pltpu
from jax.sharding import PartitionSpec as P

C = 32
S = 256
LANES = 128
F32 = jnp.float32
BF16 = jnp.bfloat16
NT = (((1,), (1,)), ((), ()))


def tile_plan(left_features, right_features, weight, bias, cotangent):
    left_rows = lax.all_gather(left_features, "col", axis=0, tiled=True)
    right_rows = lax.all_gather(right_features, "row", axis=0, tiled=True)
    row_count = left_rows.shape[0]
    col_count = right_rows.shape[0]
    out_width = weight.shape[1]
    left_block = left_rows.reshape(row_count, -1, C)
    right_block = right_rows.reshape(col_count, -1, C)
    outer_sum = jnp.einsum(
        "isc,jsd->ijcd", left_block, right_block, preferred_element_type=jnp.float32
    )
    half_mean = (outer_sum / S).astype(jnp.bfloat16).reshape(row_count * col_count, C * C)
    proj_part = jnp.dot(half_mean, weight, preferred_element_type=jnp.float32).reshape(
        row_count, col_count, out_width
    )
    pair_sum = lax.psum_scatter(proj_part, "rep", scatter_dimension=1, tiled=True)
    pair_out = pair_sum + bias
    flat_grad = cotangent.reshape(row_count * col_count, out_width)
    weight_part = jnp.einsum("pk,pe->ke", half_mean, flat_grad, preferred_element_type=jnp.float32)
    weight_grad = lax.psum(weight_part, ("row", "col", "rep"))
    grad_mean = jnp.einsum("pe,ke->pk", flat_grad, weight, preferred_element_type=jnp.float32) / S
    grad_mean = grad_mean.astype(jnp.bfloat16).reshape(row_count, col_count, C, C)
    left_part = jnp.einsum(
        "ijcd,jsd->isc", grad_mean, right_block, preferred_element_type=jnp.float32
    ).reshape(row_count, -1)
    right_part = jnp.einsum(
        "ijcd,isc->jsd", grad_mean, left_block, preferred_element_type=jnp.float32
    ).reshape(col_count, -1)
    left_sum = lax.psum_scatter(left_part, "col", scatter_dimension=0, tiled=True)
    right_sum = lax.psum_scatter(right_part, "row", scatter_dimension=0, tiled=True)
    return (pair_out, left_sum.astype(jnp.bfloat16), right_sum.astype(jnp.bfloat16), weight_grad)


def exchange(x, axis, flip, size):
    return lax.ppermute(x, axis, [(k, k ^ flip) for k in range(size)])


def swap_blocks(blocks, width):
    count = len(blocks)
    lane_block = lax.broadcasted_iota(jnp.int32, blocks[0].shape, 1) // width
    bit = 1
    while bit < count:
        upper = (lane_block & bit) != 0
        out = list(blocks)
        for a in range(count):
            if a & bit == 0:
                low, high = blocks[a], blocks[a | bit]
                out[a] = jnp.where(upper, pltpu.roll(high, bit * width, 1), low)
                out[a | bit] = jnp.where(upper, high, pltpu.roll(low, LANES - bit * width, 1))
        blocks = out
        bit *= 2
    return blocks


def pick_diagonals(blocks, width, sign):
    count = len(blocks)
    lane_block = lax.broadcasted_iota(jnp.int32, blocks[0].shape, 1) // width
    bit = 1
    while bit < count:
        upper = (lane_block & bit) != 0
        blocks = [jnp.where(upper, blocks[(m + sign * bit) % count], blocks[m]) for m in range(count)]
        bit *= 2
    return blocks


def skew_blocks(blocks, width):
    count = len(blocks)
    blocks = pick_diagonals([pltpu.roll(x, k * width, 1) if k else x for k, x in enumerate(blocks)], width, 1)
    return [blocks[-c % count] for c in range(count)]


def block_kernel(left_in, right_in, cotangent_in, bias_in, block, bias, left, right, cotangent, sems):
    pairs = ((left_in, left), (right_in, right), (cotangent_in, cotangent), (bias_in, bias))
    copies = [pltpu.make_async_copy(source, into, sems.at[k]) for k, (source, into) in enumerate(pairs)]
    for copy in copies:
        copy.start()
    for copy in copies:
        copy.wait()
    held, width = left.shape
    groups = width // LANES
    parts = [ref[t:t + 1, :].astype(F32).reshape(groups, LANES) for ref in (left, right) for t in range(held)]
    turned = jnp.concatenate(pick_diagonals(parts, C, -1), axis=0).T
    parts = pick_diagonals([turned[k * C:(k + 1) * C, :] for k in range(LANES // C)], C, 1)
    rows = [pltpu.roll(parts[-k], LANES - k * C, 1) if k else parts[0] for k in range(len(parts))]
    block[0, :LANES, :] = jnp.concatenate(rows, axis=0).astype(BF16)
    per_row, per_col, _ = cotangent.shape
    cot = cotangent[...].astype(F32)
    parts = [cot[:, j, :] for j in range(per_col)]
    block[0, LANES:, :] = jnp.concatenate(parts, axis=0).astype(BF16)


def turn_back(rows, scratch, left_grad, right_grad):
    held, width = left_grad.shape
    groups = width // LANES
    blocks = swap_blocks([rows[k * C:(k + 1) * C, :] for k in range(LANES // C)], C)
    scratch[...] = jnp.concatenate(blocks, axis=0).T
    for at, ref in ((0, left_grad), (held * groups, right_grad)):
        for g in range(groups):
            ref[:, g * LANES:(g + 1) * LANES] = scratch[pl.ds(at + g, held, stride=groups), :].astype(BF16)


def spread(source, col, slots, first, into, stride):
    for slot in range(slots):
        for t in range(2):
            at = (col ^ slot) * 2 + t
            into[pl.ds(at, C, stride=stride), :] = source[slot, first + t * C:first + (t + 1) * C, :].astype(F32)


def spread_cot(source, col, slots, rows, into):
    per_row = 2 * slots
    for slot in range(slots):
        cot = source[slot, 4 * C:, :].astype(F32)
        for j in range(2 * rows):
            at = pl.multiple_of(((col ^ slot) * 2 + j % 2) * per_row, per_row)
            into[j // 2, pl.ds(at, per_row), :] = cot[j * per_row:(j + 1) * per_row, :]


def mixing_rows(outer_weight, cot_rows):
    tokens = cot_rows[0].shape[0]
    copies = LANES // tokens
    repeated = jnp.concatenate([jnp.concatenate([rows] * copies, axis=0) for rows in cot_rows], axis=0).astype(BF16)
    grads = lax.dot_general(outer_weight, repeated, NT, preferred_element_type=F32)
    copy_of = lax.broadcasted_iota(jnp.int32, (C, LANES), 1) // tokens
    out = []
    for two in range(2):
        lanes = grads[:, two * LANES:(two + 1) * LANES]
        parts = []
        for group in range(C // copies):
            first = group * copies * C
            part = lanes[first:first + C, :]
            for k in range(1, copies):
                at = first + k * C
                part = jnp.where(copy_of == k, lanes[at:at + C, :], part)
            parts.append((part * (1.0 / S)).astype(BF16))
        out.append(jnp.concatenate(parts, axis=1))
    return jnp.concatenate(out, axis=0)


def left_cots(cot, half, col, slots):
    per_row = 2 * slots
    return [cot[half, pl.ds(col * 2 + t, per_row, stride=per_row), :] for t in range(2)]


def right_cots(cot, half, col, slots):
    per_row = 2 * slots
    return [cot[half, pl.ds(pl.multiple_of((col * 2 + t) * per_row, per_row), per_row), :] for t in range(2)]


def near_kernel(rows, near, weight, sent, lefts, cot, grads, far_mix, spread_right, weight_dc):
    slots = near.shape[0]
    row, col = lax.axis_index("row"), lax.axis_index("col")
    tokens = 2 * slots
    spread(near, col, slots, 0, lefts, tokens)
    spread(near, col, slots, 2 * C, spread_right, tokens)
    spread_cot(near, col, slots, rows, cot)
    span = tokens * C
    sent[:span, :] = lefts[...].astype(BF16)
    for slot in range(slots):
        sent[pl.ds(pl.multiple_of(span + (col ^ slot) * 2 * C, 2 * C), 2 * C), :] = near[slot, 2 * C:4 * C, :]
    all_weight = weight[...]
    weight_dc[...] = jnp.swapaxes(all_weight.astype(F32).reshape(C, C, LANES), 0, 1).reshape(C * C, LANES).astype(BF16)
    mix = mixing_rows(weight_dc[...], left_cots(cot, row, col, slots))
    grads[:2 * C, :] = jnp.dot(mix, spread_right[...].astype(BF16), preferred_element_type=F32)
    far_mix[...] = mixing_rows(weight_dc[...], left_cots(cot, 1 - row, col, slots))
    mix = mixing_rows(all_weight, right_cots(cot, row, col, slots))
    grads[2 * C:, :] = jnp.dot(mix, lefts[...].astype(BF16), preferred_element_type=F32)


def ordered(first, near, far):
    return jnp.concatenate([jnp.where(first, near, far), jnp.where(first, far, near)], axis=1)


def far_kernel(
    rows, far, near, near_lefts, near_cot, near_grads, far_mix, weight,
    lefts, rights, cot_all, left_grad, right_grad, far_lefts, far_cot, spread_right, turned,
):
    slots = far.shape[0]
    row, col = lax.axis_index("row"), lax.axis_index("col")
    per_row = 2 * slots
    tokens = rows * per_row
    spread(far, col, slots, 0, far_lefts, per_row)
    spread(far, col, slots, 2 * C, spread_right, per_row)
    spread_cot(far, col, slots, rows, far_cot)
    left = jnp.dot(far_mix[...], spread_right[...].astype(BF16), preferred_element_type=F32)
    mix = mixing_rows(weight[...], right_cots(far_cot, row, col, slots))
    right = jnp.dot(mix, far_lefts[...].astype(BF16), preferred_element_type=F32)
    turn_back(near_grads[...] + jnp.concatenate([left, right], axis=0), turned, left_grad, right_grad)
    first = row == 0
    both = ordered(first, near_lefts[...].reshape(C, per_row, LANES), far_lefts[...].reshape(C, per_row, LANES))
    lefts[...] = both.reshape(C * tokens, LANES).astype(BF16)
    sort_rights(near, far, row, col, slots, rows, 2 * C, rights)
    for q in range(slots):
        at = slice(q * 2 * per_row, (q + 1) * 2 * per_row)
        for half in range(rows):
            near_rows = near_cot[half, at, :].reshape(2, per_row, LANES)
            both = ordered(first, near_rows, far_cot[half, at, :].reshape(2, per_row, LANES))
            first_row = (q * rows + half) * 2 * tokens
            cot_all[first_row:first_row + 2 * tokens, :] = both.reshape(2 * tokens, LANES).astype(BF16)


def sort_rights(near, far, row, col, slots, rows, first, into):
    for half, source in enumerate((near, far)):
        for slot in range(slots):
            chip = (col ^ slot) * rows + lax.rem(row + half, rows)
            into[pl.ds(pl.multiple_of(chip * 2 * C, 2 * C), 2 * C), :] = source[slot, first:first + 2 * C, :]


def outer_kernel(
    rows, slots, near_sent, own_lefts, own_rights, other, cot_all, weight, bias, left_in, right_in,
    pair_out, left_out, right_out, weight_out, spread_left, lefts, rights, pair_block, weight_grad, sems,
):
    row, col, rep = lax.axis_index("row"), lax.axis_index("col"), lax.axis_index("rep")
    copies = [
        pltpu.make_async_copy(left_in, left_out, sems.at[0]),
        pltpu.make_async_copy(right_in, right_out, sems.at[1]),
    ]
    for copy in copies:
        copy.start()
    per_row, per_col = 2 * slots, 2 * rows
    tokens = rows * per_row
    span = per_row * C
    stride = (other.shape[0] - 2 * span) // slots
    for slot in range(slots):
        for t in range(2):
            at = 2 * span + slot * stride + t * C
            spread_left[pl.ds((col ^ slot) * 2 + t, C, stride=per_row), :] = other[at:at + C, :].astype(F32)
    near = other[:span, :].astype(F32).reshape(C, per_row, LANES)
    both = ordered(row == 0, near, spread_left[...].reshape(C, per_row, LANES))
    lefts[rep] = own_lefts[...]
    lefts[1 - rep] = both.reshape(C * tokens, LANES).astype(BF16)
    rights[rep] = own_rights[...]
    for q in range(slots):
        at = pl.multiple_of((q * rows + row) * 2 * C, 2 * C)
        rights[1 - rep, pl.ds(at, 2 * C), :] = other[span + q * 2 * C:span + (q + 1) * 2 * C, :]
        at = pl.multiple_of(((col ^ q) * rows + 1 - row) * 2 * C, 2 * C)
        rights[1 - rep, pl.ds(at, 2 * C), :] = other[2 * span + q * stride + 2 * C:2 * span + q * stride + 4 * C, :]

    def all_of(ref, at):
        return jnp.concatenate([ref[0, at, :], ref[1, at, :]], axis=1)

    right_all = all_of(rights, slice(None))
    count = LANES // tokens
    groups = C // count
    means = [[[] for _ in range(groups)] for _ in range(count)]
    for g in range(groups):
        if g % 2 == 0:
            left = all_of(lefts, slice(g * LANES, (g + 2) * LANES))
            wide = lax.dot_general(right_all, left, NT, preferred_element_type=F32) * (1.0 / S)
        outer = wide[:, g % 2 * LANES:(g % 2 + 1) * LANES]
        for h in range(tokens // count):
            first = h * count * C
            blocks = [outer[first + k * C:first + (k + 1) * C, :] for k in range(count)]
            for c, mean in enumerate(skew_blocks(blocks, tokens)):
                means[c][g].append(mean)
    own_count = per_col // 2
    at = pl.ds(pl.multiple_of((col * per_col + rep * own_count) * C, own_count * C), own_count * C)
    own_left = jnp.concatenate([near_sent[:span, :], other[:span, :]], axis=1)
    own_right = jnp.concatenate([rights[rep, at, :], rights[1 - rep, at, :]], axis=1)
    own = lax.dot_general(own_left, own_right, NT, preferred_element_type=F32) * (1.0 / S)
    own_mean = jnp.concatenate(
        [
            jnp.concatenate([own[c * per_row:(c + 1) * per_row, t * C:(t + 1) * C] for c in range(C)], axis=1)
            for t in range(own_count)
        ],
        axis=0,
    ).astype(BF16)
    own_pairs = jnp.dot(own_mean, weight[...], preferred_element_type=F32) + bias[...]
    for t in range(own_count):
        pair_block[:, t, :] = own_pairs[t * per_row:(t + 1) * per_row, :]
    copy = pltpu.make_async_copy(pair_block, pair_out, sems.at[2])
    copy.start()
    copies.append(copy)
    for c in range(count):
        mean = jnp.concatenate([jnp.concatenate(halves, axis=1) for halves in means[c]], axis=0).astype(BF16)
        cot = jnp.concatenate(
            [
                cot_all[at:at + tokens, :]
                for h in range(tokens // count)
                for at in [(h * count + (k - c) % count) * tokens for k in range(count)]
            ],
            axis=0,
        )
        part = jnp.dot(mean, cot, preferred_element_type=F32)
        at = slice(c * C, (c + 1) * C)
        weight_grad[:, at, :] = part.reshape(groups, C, LANES)
        copy = pltpu.make_async_copy(weight_grad.at[:, at], weight_out.at[:, at], sems.at[3 + c])
        copy.start()
        copies.append(copy)

    for copy in copies:
        copy.wait()


def gather_plan(rows, cols, left_features, right_features, weight, bias, cotangent):
    held, width = left_features.shape
    seqs = width // C
    tokens = held * rows * cols
    half_span = tokens // rows * C
    per_row, per_col, e = cotangent.shape
    vmem = pl.BlockSpec(memory_space=pltpu.VMEM)
    anywhere = pl.BlockSpec(memory_space=pl.ANY)
    params = pltpu.CompilerParams(vmem_limit_bytes=32 * 1024 * 1024)
    array = jax.ShapeDtypeStruct

    in_hbm = [left_features, right_features, cotangent, bias.reshape(1, e)]
    block, bias_row = pl.pallas_call(
        block_kernel,
        out_shape=(array((1, 2 * held * C + per_row * per_col, seqs), BF16), array((1, e), F32)),
        in_specs=[pl.BlockSpec(memory_space=pltpu.HBM)] * 4,
        out_specs=(vmem, vmem),
        scratch_shapes=[
            pltpu.VMEM((held, width), BF16),
            pltpu.VMEM((held, width), BF16),
            pltpu.VMEM((per_row, per_col, e), BF16),
            pltpu.SemaphoreType.DMA((4,)),
        ],
        compiler_params=params,
        name="own_block",
    )(*(pltpu.with_memory_space_constraint(x, pltpu.HBM) for x in in_hbm))
    flip = 1
    while flip < cols:
        arrived = exchange(block, "col", flip, cols)
        if flip * 2 == cols:
            far = [exchange(block, "row", 1, rows), exchange(arrived, "row", 1, rows)]
        block = jnp.concatenate([block, arrived], axis=0)
        flip *= 2
    far = jnp.concatenate(far, axis=0)

    lefts = array((half_span, seqs), F32)
    cots = array((rows, cols * held * per_row, e), F32)
    near_sent, near_lefts, near_cot, near_grads, far_mix = pl.pallas_call(
        functools.partial(near_kernel, rows),
        out_shape=(
            array((2 * half_span, seqs), BF16),
            lefts,
            cots,
            array((2 * held * C, seqs), F32),
            array((held * C, half_span), BF16),
        ),
        in_specs=[vmem] * 2,
        out_specs=(vmem,) * 5,
        scratch_shapes=[pltpu.VMEM((half_span, seqs), F32), pltpu.VMEM((C * C, e), BF16)],
        compiler_params=params,
        cost_estimate=pl.CostEstimate(flops=300_000_000, bytes_accessed=2_000_000, transcendentals=0),
        name="near_part",
    )(block, weight)
    other = exchange(jnp.concatenate([near_sent, far.reshape(-1, seqs)], axis=0), "rep", 1, 2)

    own_lefts, own_rights, cot_all, left_grad, right_grad = pl.pallas_call(
        functools.partial(far_kernel, rows),
        out_shape=(
            array((tokens * C, seqs), BF16),
            array((tokens * C, seqs), BF16),
            array((tokens * tokens, e), BF16),
            array((held, width), BF16),
            array((held, width), BF16),
        ),
        in_specs=[vmem] * 7,
        out_specs=(vmem,) * 5,
        scratch_shapes=[
            pltpu.VMEM((half_span, seqs), F32),
            pltpu.VMEM(cots.shape, F32),
            pltpu.VMEM((half_span, seqs), F32),
            pltpu.VMEM((LANES, LANES), F32),
        ],
        compiler_params=params,
        cost_estimate=pl.CostEstimate(flops=10_000_000_000, bytes_accessed=1_000_000, transcendentals=0),
        name="far_part",
    )(far, block, near_lefts, near_cot, near_grads, far_mix, weight)

    split = (C * tokens // LANES, LANES // tokens * C, e)
    pair_out, left_grad, right_grad, weight_grad = pl.pallas_call(
        functools.partial(outer_kernel, rows, cols),
        out_shape=(
            array((per_row, per_col // 2, e), F32),
            array((held, width), BF16),
            array((held, width), BF16),
            array(split, F32),
        ),
        in_specs=[vmem] * 9,
        out_specs=(anywhere,) * 4,
        scratch_shapes=[
            pltpu.VMEM((half_span, seqs), F32),
            pltpu.VMEM((2, tokens * C, seqs), BF16),
            pltpu.VMEM((2, tokens * C, seqs), BF16),
            pltpu.VMEM((per_row, per_col // 2, e), F32),
            pltpu.VMEM(split, F32),
            pltpu.SemaphoreType.DMA((3 + LANES // tokens,)),
        ],
        compiler_params=params,
        name="outer_mean",
    )(near_sent, own_lefts, own_rights, other, cot_all, weight, bias_row, left_grad, right_grad)
    return pair_out, left_grad, right_grad, weight_grad.reshape(C * C, e)


def solution(mesh):
    rows, cols = mesh.shape["row"], mesh.shape["col"]

    def on_device(left_features, right_features, weight, bias, cotangent):
        held, width = left_features.shape
        tokens = held * rows * cols
        small = held == 2 and rows == 2 and cols & (cols - 1) == 0 and LANES % tokens == 0 and tokens == 16
        if small and width == LANES * C and weight.shape[1] == LANES and C % (LANES // tokens) == 0:
            return gather_plan(rows, cols, left_features, right_features, weight, bias, cotangent)
        return tile_plan(left_features, right_features, weight, bias, cotangent)

    in_specs = (
        P(("groups", "row", "col"), "rep"),
        P(("groups", "col", "row"), "rep"),
        P(),
        P(),
        P(("groups", "row"), "col", None),
    )
    out_specs = (
        P(("groups", "row"), ("col", "rep"), None),
        P(("groups", "row", "col"), "rep"),
        P(("groups", "col", "row"), "rep"),
        P("groups", None),
    )
    return jax.shard_map(
        on_device, mesh=mesh, in_specs=in_specs, out_specs=out_specs, check_vma=False
    )
```

```python
import functools

import jax
import jax.numpy as jnp
from jax import lax
from jax.experimental import pallas as pl
from jax.experimental.pallas import tpu as pltpu
from jax.sharding import PartitionSpec as P

C = 32
S = 256
LANES = 128
F32 = jnp.float32
BF16 = jnp.bfloat16
NT = (((1,), (1,)), ((), ()))


def tile_plan(left_features, right_features, weight, bias, cotangent):
    left_rows = lax.all_gather(left_features, "col", axis=0, tiled=True)
    right_rows = lax.all_gather(right_features, "row", axis=0, tiled=True)
    row_count = left_rows.shape[0]
    col_count = right_rows.shape[0]
    out_width = weight.shape[1]
    left_block = left_rows.reshape(row_count, -1, C)
    right_block = right_rows.reshape(col_count, -1, C)
    outer_sum = jnp.einsum(
        "isc,jsd->ijcd", left_block, right_block, preferred_element_type=jnp.float32
    )
    half_mean = (outer_sum / S).astype(jnp.bfloat16).reshape(row_count * col_count, C * C)
    proj_part = jnp.dot(half_mean, weight, preferred_element_type=jnp.float32).reshape(
        row_count, col_count, out_width
    )
    pair_sum = lax.psum_scatter(proj_part, "rep", scatter_dimension=1, tiled=True)
    pair_out = pair_sum + bias
    flat_grad = cotangent.reshape(row_count * col_count, out_width)
    weight_part = jnp.einsum("pk,pe->ke", half_mean, flat_grad, preferred_element_type=jnp.float32)
    weight_grad = lax.psum(weight_part, ("row", "col", "rep"))
    grad_mean = jnp.einsum("pe,ke->pk", flat_grad, weight, preferred_element_type=jnp.float32) / S
    grad_mean = grad_mean.astype(jnp.bfloat16).reshape(row_count, col_count, C, C)
    left_part = jnp.einsum(
        "ijcd,jsd->isc", grad_mean, right_block, preferred_element_type=jnp.float32
    ).reshape(row_count, -1)
    right_part = jnp.einsum(
        "ijcd,isc->jsd", grad_mean, left_block, preferred_element_type=jnp.float32
    ).reshape(col_count, -1)
    left_sum = lax.psum_scatter(left_part, "col", scatter_dimension=0, tiled=True)
    right_sum = lax.psum_scatter(right_part, "row", scatter_dimension=0, tiled=True)
    return (pair_out, left_sum.astype(jnp.bfloat16), right_sum.astype(jnp.bfloat16), weight_grad)


def exchange(x, axis, flip, size):
    return lax.ppermute(x, axis, [(k, k ^ flip) for k in range(size)])


def swap_blocks(blocks, width):
    count = len(blocks)
    lane_block = lax.broadcasted_iota(jnp.int32, blocks[0].shape, 1) // width
    bit = 1
    while bit < count:
        upper = (lane_block & bit) != 0
        out = list(blocks)
        for a in range(count):
            if a & bit == 0:
                low, high = blocks[a], blocks[a | bit]
                out[a] = jnp.where(upper, pltpu.roll(high, bit * width, 1), low)
                out[a | bit] = jnp.where(upper, high, pltpu.roll(low, LANES - bit * width, 1))
        blocks = out
        bit *= 2
    return blocks


def pick_diagonals(blocks, width, sign):
    count = len(blocks)
    lane_block = lax.broadcasted_iota(jnp.int32, blocks[0].shape, 1) // width
    bit = 1
    while bit < count:
        upper = (lane_block & bit) != 0
        blocks = [jnp.where(upper, blocks[(m + sign * bit) % count], blocks[m]) for m in range(count)]
        bit *= 2
    return blocks


def skew_blocks(blocks, width):
    count = len(blocks)
    blocks = pick_diagonals([pltpu.roll(x, k * width, 1) if k else x for k, x in enumerate(blocks)], width, 1)
    return [blocks[-c % count] for c in range(count)]


def block_kernel(left_in, right_in, cotangent_in, bias_in, block, bias, left, right, cotangent, sems):
    pairs = ((left_in, left), (right_in, right), (cotangent_in, cotangent), (bias_in, bias))
    copies = [pltpu.make_async_copy(source, into, sems.at[k]) for k, (source, into) in enumerate(pairs)]
    for copy in copies:
        copy.start()
    for copy in copies:
        copy.wait()
    held, width = left.shape
    groups = width // LANES
    parts = [ref[t:t + 1, :].astype(F32).reshape(groups, LANES) for ref in (left, right) for t in range(held)]
    turned = jnp.concatenate(pick_diagonals(parts, C, -1), axis=0).T
    parts = pick_diagonals([turned[k * C:(k + 1) * C, :] for k in range(LANES // C)], C, 1)
    rows = [pltpu.roll(parts[-k], LANES - k * C, 1) if k else parts[0] for k in range(len(parts))]
    block[0, :LANES, :] = jnp.concatenate(rows, axis=0).astype(BF16)
    per_row, per_col, _ = cotangent.shape
    cot = cotangent[...].astype(F32)
    parts = [cot[:, j, :] for j in range(per_col)]
    block[0, LANES:, :] = jnp.concatenate(parts, axis=0).astype(BF16)


def turn_back(rows, scratch, left_grad, right_grad):
    held, width = left_grad.shape
    groups = width // LANES
    blocks = swap_blocks([rows[k * C:(k + 1) * C, :] for k in range(LANES // C)], C)
    scratch[...] = jnp.concatenate(blocks, axis=0).T
    for at, ref in ((0, left_grad), (held * groups, right_grad)):
        for g in range(groups):
            ref[:, g * LANES:(g + 1) * LANES] = scratch[pl.ds(at + g, held, stride=groups), :].astype(BF16)


def spread(source, col, slots, first, into, stride):
    for slot in range(slots):
        for t in range(2):
            at = (col ^ slot) * 2 + t
            into[pl.ds(at, C, stride=stride), :] = source[slot, first + t * C:first + (t + 1) * C, :].astype(F32)


def spread_cot(source, col, slots, rows, into):
    per_row = 2 * slots
    for slot in range(slots):
        cot = source[slot, 4 * C:, :].astype(F32)
        for j in range(2 * rows):
            at = pl.multiple_of(((col ^ slot) * 2 + j % 2) * per_row, per_row)
            into[j // 2, pl.ds(at, per_row), :] = cot[j * per_row:(j + 1) * per_row, :]


def mixing_rows(outer_weight, cot_rows):
    tokens = cot_rows[0].shape[0]
    copies = LANES // tokens
    repeated = jnp.concatenate([jnp.concatenate([rows] * copies, axis=0) for rows in cot_rows], axis=0).astype(BF16)
    grads = lax.dot_general(outer_weight, repeated, NT, preferred_element_type=F32)
    copy_of = lax.broadcasted_iota(jnp.int32, (C, LANES), 1) // tokens
    out = []
    for two in range(2):
        lanes = grads[:, two * LANES:(two + 1) * LANES]
        parts = []
        for group in range(C // copies):
            first = group * copies * C
            part = lanes[first:first + C, :]
            for k in range(1, copies):
                at = first + k * C
                part = jnp.where(copy_of == k, lanes[at:at + C, :], part)
            parts.append((part * (1.0 / S)).astype(BF16))
        out.append(jnp.concatenate(parts, axis=1))
    return jnp.concatenate(out, axis=0)


def left_cots(cot, half, col, slots):
    per_row = 2 * slots
    return [cot[half, pl.ds(col * 2 + t, per_row, stride=per_row), :] for t in range(2)]


def right_cots(cot, half, col, slots):
    per_row = 2 * slots
    return [cot[half, pl.ds(pl.multiple_of((col * 2 + t) * per_row, per_row), per_row), :] for t in range(2)]


def near_kernel(rows, near, weight, sent, lefts, cot, grads, far_mix, spread_right, weight_dc):
    slots = near.shape[0]
    row, col = lax.axis_index("row"), lax.axis_index("col")
    tokens = 2 * slots
    spread(near, col, slots, 0, lefts, tokens)
    spread(near, col, slots, 2 * C, spread_right, tokens)
    spread_cot(near, col, slots, rows, cot)
    span = tokens * C
    sent[:span, :] = lefts[...].astype(BF16)
    for slot in range(slots):
        sent[pl.ds(pl.multiple_of(span + (col ^ slot) * 2 * C, 2 * C), 2 * C), :] = near[slot, 2 * C:4 * C, :]
    all_weight = weight[...]
    weight_dc[...] = jnp.swapaxes(all_weight.astype(F32).reshape(C, C, LANES), 0, 1).reshape(C * C, LANES).astype(BF16)
    mix = mixing_rows(weight_dc[...], left_cots(cot, row, col, slots))
    grads[:2 * C, :] = jnp.dot(mix, spread_right[...].astype(BF16), preferred_element_type=F32)
    far_mix[...] = mixing_rows(weight_dc[...], left_cots(cot, 1 - row, col, slots))
    mix = mixing_rows(all_weight, right_cots(cot, row, col, slots))
    grads[2 * C:, :] = jnp.dot(mix, lefts[...].astype(BF16), preferred_element_type=F32)


def ordered(first, near, far):
    return jnp.concatenate([jnp.where(first, near, far), jnp.where(first, far, near)], axis=1)


def far_kernel(
    rows, far, near, near_lefts, near_cot, near_grads, far_mix, weight,
    lefts, rights, cot_all, left_grad, right_grad, far_lefts, far_cot, spread_right, turned,
):
    slots = far.shape[0]
    row, col = lax.axis_index("row"), lax.axis_index("col")
    per_row = 2 * slots
    tokens = rows * per_row
    spread(far, col, slots, 0, far_lefts, per_row)
    spread(far, col, slots, 2 * C, spread_right, per_row)
    spread_cot(far, col, slots, rows, far_cot)
    left = jnp.dot(far_mix[...], spread_right[...].astype(BF16), preferred_element_type=F32)
    mix = mixing_rows(weight[...], right_cots(far_cot, row, col, slots))
    right = jnp.dot(mix, far_lefts[...].astype(BF16), preferred_element_type=F32)
    turn_back(near_grads[...] + jnp.concatenate([left, right], axis=0), turned, left_grad, right_grad)
    first = row == 0
    both = ordered(first, near_lefts[...].reshape(C, per_row, LANES), far_lefts[...].reshape(C, per_row, LANES))
    lefts[...] = both.reshape(C * tokens, LANES).astype(BF16)
    sort_rights(near, far, row, col, slots, rows, 2 * C, rights)
    for q in range(slots):
        at = slice(q * 2 * per_row, (q + 1) * 2 * per_row)
        for half in range(rows):
            near_rows = near_cot[half, at, :].reshape(2, per_row, LANES)
            both = ordered(first, near_rows, far_cot[half, at, :].reshape(2, per_row, LANES))
            first_row = (q * rows + half) * 2 * tokens
            cot_all[first_row:first_row + 2 * tokens, :] = both.reshape(2 * tokens, LANES).astype(BF16)


def sort_rights(near, far, row, col, slots, rows, first, into):
    for half, source in enumerate((near, far)):
        for slot in range(slots):
            chip = (col ^ slot) * rows + lax.rem(row + half, rows)
            into[pl.ds(pl.multiple_of(chip * 2 * C, 2 * C), 2 * C), :] = source[slot, first:first + 2 * C, :]


def outer_kernel(
    rows, slots, near_sent, own_lefts, own_rights, other, cot_all, weight, bias, left_in, right_in,
    pair_out, left_out, right_out, weight_out, spread_left, lefts, rights, pair_block, weight_grad, sems,
):
    row, col, rep = lax.axis_index("row"), lax.axis_index("col"), lax.axis_index("rep")
    copies = [
        pltpu.make_async_copy(left_in, left_out, sems.at[0]),
        pltpu.make_async_copy(right_in, right_out, sems.at[1]),
    ]
    for copy in copies:
        copy.start()
    per_row, per_col = 2 * slots, 2 * rows
    tokens = rows * per_row
    span = per_row * C
    stride = (other.shape[0] - 2 * span) // slots
    for slot in range(slots):
        for t in range(2):
            at = 2 * span + slot * stride + t * C
            spread_left[pl.ds((col ^ slot) * 2 + t, C, stride=per_row), :] = other[at:at + C, :].astype(F32)
    near = other[:span, :].astype(F32).reshape(C, per_row, LANES)
    both = ordered(row == 0, near, spread_left[...].reshape(C, per_row, LANES))
    lefts[rep] = own_lefts[...]
    lefts[1 - rep] = both.reshape(C * tokens, LANES).astype(BF16)
    rights[rep] = own_rights[...]
    for q in range(slots):
        at = pl.multiple_of((q * rows + row) * 2 * C, 2 * C)
        rights[1 - rep, pl.ds(at, 2 * C), :] = other[span + q * 2 * C:span + (q + 1) * 2 * C, :]
        at = pl.multiple_of(((col ^ q) * rows + 1 - row) * 2 * C, 2 * C)
        rights[1 - rep, pl.ds(at, 2 * C), :] = other[2 * span + q * stride + 2 * C:2 * span + q * stride + 4 * C, :]

    def all_of(ref, at):
        return jnp.concatenate([ref[0, at, :], ref[1, at, :]], axis=1)

    right_all = all_of(rights, slice(None))
    count = LANES // tokens
    groups = C // count
    means = [[[] for _ in range(groups)] for _ in range(count)]
    for g in range(groups):
        if g % 2 == 0:
            left = all_of(lefts, slice(g * LANES, (g + 2) * LANES))
            wide = lax.dot_general(right_all, left, NT, preferred_element_type=F32) * (1.0 / S)
        outer = wide[:, g % 2 * LANES:(g % 2 + 1) * LANES]
        for h in range(tokens // count):
            first = h * count * C
            blocks = [outer[first + k * C:first + (k + 1) * C, :] for k in range(count)]
            for c, mean in enumerate(skew_blocks(blocks, tokens)):
                means[c][g].append(mean)
    own_count = per_col // 2
    at = pl.ds(pl.multiple_of((col * per_col + rep * own_count) * C, own_count * C), own_count * C)
    own_left = jnp.concatenate([near_sent[:span, :], other[:span, :]], axis=1)
    own_right = jnp.concatenate([rights[rep, at, :], rights[1 - rep, at, :]], axis=1)
    own = lax.dot_general(own_left, own_right, NT, preferred_element_type=F32) * (1.0 / S)
    own_mean = jnp.concatenate(
        [
            jnp.concatenate([own[c * per_row:(c + 1) * per_row, t * C:(t + 1) * C] for c in range(C)], axis=1)
            for t in range(own_count)
        ],
        axis=0,
    ).astype(BF16)
    own_pairs = jnp.dot(own_mean, weight[...], preferred_element_type=F32) + bias[...]
    for t in range(own_count):
        pair_block[:, t, :] = own_pairs[t * per_row:(t + 1) * per_row, :]
    copy = pltpu.make_async_copy(pair_block, pair_out, sems.at[2])
    copy.start()
    copies.append(copy)
    for c in range(count):
        mean = jnp.concatenate([jnp.concatenate(halves, axis=1) for halves in means[c]], axis=0).astype(BF16)
        cot = jnp.concatenate(
            [
                cot_all[at:at + tokens, :]
                for h in range(tokens // count)
                for at in [(h * count + (k - c) % count) * tokens for k in range(count)]
            ],
            axis=0,
        )
        part = jnp.dot(mean, cot, preferred_element_type=F32)
        at = slice(c * C, (c + 1) * C)
        weight_grad[:, at, :] = part.reshape(groups, C, LANES)
        copy = pltpu.make_async_copy(weight_grad.at[:, at], weight_out.at[:, at], sems.at[3 + c])
        copy.start()
        copies.append(copy)

    for copy in copies:
        copy.wait()


def gather_plan(rows, cols, left_features, right_features, weight, bias, cotangent):
    held, width = left_features.shape
    seqs = width // C
    tokens = held * rows * cols
    half_span = tokens // rows * C
    per_row, per_col, e = cotangent.shape
    vmem = pl.BlockSpec(memory_space=pltpu.VMEM)
    anywhere = pl.BlockSpec(memory_space=pl.ANY)
    params = pltpu.CompilerParams(vmem_limit_bytes=32 * 1024 * 1024)
    array = jax.ShapeDtypeStruct

    in_hbm = [left_features, right_features, cotangent, bias.reshape(1, e)]
    block, bias_row = pl.pallas_call(
        block_kernel,
        out_shape=(array((1, 2 * held * C + per_row * per_col, seqs), BF16), array((1, e), F32)),
        in_specs=[pl.BlockSpec(memory_space=pltpu.HBM)] * 4,
        out_specs=(vmem, vmem),
        scratch_shapes=[
            pltpu.VMEM((held, width), BF16),
            pltpu.VMEM((held, width), BF16),
            pltpu.VMEM((per_row, per_col, e), BF16),
            pltpu.SemaphoreType.DMA((4,)),
        ],
        compiler_params=params,
        name="own_block",
    )(*(pltpu.with_memory_space_constraint(x, pltpu.HBM) for x in in_hbm))
    flip = 1
    while flip < cols:
        arrived = exchange(block, "col", flip, cols)
        if flip * 2 == cols:
            far = [exchange(block, "row", 1, rows), exchange(arrived, "row", 1, rows)]
        block = jnp.concatenate([block, arrived], axis=0)
        flip *= 2
    far = jnp.concatenate(far, axis=0)

    lefts = array((half_span, seqs), F32)
    cots = array((rows, cols * held * per_row, e), F32)
    near_sent, near_lefts, near_cot, near_grads, far_mix = pl.pallas_call(
        functools.partial(near_kernel, rows),
        out_shape=(
            array((2 * half_span, seqs), BF16),
            lefts,
            cots,
            array((2 * held * C, seqs), F32),
            array((held * C, half_span), BF16),
        ),
        in_specs=[vmem] * 2,
        out_specs=(vmem,) * 5,
        scratch_shapes=[pltpu.VMEM((half_span, seqs), F32), pltpu.VMEM((C * C, e), BF16)],
        compiler_params=params,
        cost_estimate=pl.CostEstimate(flops=300_000_000, bytes_accessed=2_000_000, transcendentals=0),
        name="near_part",
    )(block, weight)
    other = exchange(jnp.concatenate([near_sent, far[:, :2 * held * C].reshape(-1, seqs)], axis=0), "rep", 1, 2)

    own_lefts, own_rights, cot_all, left_grad, right_grad = pl.pallas_call(
        functools.partial(far_kernel, rows),
        out_shape=(
            array((tokens * C, seqs), BF16),
            array((tokens * C, seqs), BF16),
            array((tokens * tokens, e), BF16),
            array((held, width), BF16),
            array((held, width), BF16),
        ),
        in_specs=[vmem] * 7,
        out_specs=(vmem,) * 5,
        scratch_shapes=[
            pltpu.VMEM((half_span, seqs), F32),
            pltpu.VMEM(cots.shape, F32),
            pltpu.VMEM((half_span, seqs), F32),
            pltpu.VMEM((LANES, LANES), F32),
        ],
        compiler_params=params,
        cost_estimate=pl.CostEstimate(flops=10_000_000_000, bytes_accessed=1_000_000, transcendentals=0),
        name="far_part",
    )(far, block, near_lefts, near_cot, near_grads, far_mix, weight)

    split = (C * tokens // LANES, LANES // tokens * C, e)
    pair_out, left_grad, right_grad, weight_grad = pl.pallas_call(
        functools.partial(outer_kernel, rows, cols),
        out_shape=(
            array((per_row, per_col // 2, e), F32),
            array((held, width), BF16),
            array((held, width), BF16),
            array(split, F32),
        ),
        in_specs=[vmem] * 9,
        out_specs=(anywhere,) * 4,
        scratch_shapes=[
            pltpu.VMEM((half_span, seqs), F32),
            pltpu.VMEM((2, tokens * C, seqs), BF16),
            pltpu.VMEM((2, tokens * C, seqs), BF16),
            pltpu.VMEM((per_row, per_col // 2, e), F32),
            pltpu.VMEM(split, F32),
            pltpu.SemaphoreType.DMA((3 + LANES // tokens,)),
        ],
        compiler_params=params,
        name="outer_mean",
    )(near_sent, own_lefts, own_rights, other, cot_all, weight, bias_row, left_grad, right_grad)
    return pair_out, left_grad, right_grad, weight_grad.reshape(C * C, e)


def solution(mesh):
    rows, cols = mesh.shape["row"], mesh.shape["col"]

    def on_device(left_features, right_features, weight, bias, cotangent):
        held, width = left_features.shape
        tokens = held * rows * cols
        small = held == 2 and rows == 2 and cols & (cols - 1) == 0 and LANES % tokens == 0 and tokens == 16
        if small and width == LANES * C and weight.shape[1] == LANES and C % (LANES // tokens) == 0:
            return gather_plan(rows, cols, left_features, right_features, weight, bias, cotangent)
        return tile_plan(left_features, right_features, weight, bias, cotangent)

    in_specs = (
        P(("groups", "row", "col"), "rep"),
        P(("groups", "col", "row"), "rep"),
        P(),
        P(),
        P(("groups", "row"), "col", None),
    )
    out_specs = (
        P(("groups", "row"), ("col", "rep"), None),
        P(("groups", "row", "col"), "rep"),
        P(("groups", "col", "row"), "rep"),
        P("groups", None),
    )
    return jax.shard_map(
        on_device, mesh=mesh, in_specs=in_specs, out_specs=out_specs, check_vma=False
    )
```

```python
import functools

import jax
import jax.numpy as jnp
from jax import lax
from jax.experimental import pallas as pl
from jax.experimental.pallas import tpu as pltpu
from jax.sharding import PartitionSpec as P

C = 32
S = 256
LANES = 128
F32 = jnp.float32
BF16 = jnp.bfloat16
NT = (((1,), (1,)), ((), ()))


def tile_plan(left_features, right_features, weight, bias, cotangent):
    left_rows = lax.all_gather(left_features, "col", axis=0, tiled=True)
    right_rows = lax.all_gather(right_features, "row", axis=0, tiled=True)
    row_count = left_rows.shape[0]
    col_count = right_rows.shape[0]
    out_width = weight.shape[1]
    left_block = left_rows.reshape(row_count, -1, C)
    right_block = right_rows.reshape(col_count, -1, C)
    outer_sum = jnp.einsum(
        "isc,jsd->ijcd", left_block, right_block, preferred_element_type=jnp.float32
    )
    half_mean = (outer_sum / S).astype(jnp.bfloat16).reshape(row_count * col_count, C * C)
    proj_part = jnp.dot(half_mean, weight, preferred_element_type=jnp.float32).reshape(
        row_count, col_count, out_width
    )
    pair_sum = lax.psum_scatter(proj_part, "rep", scatter_dimension=1, tiled=True)
    pair_out = pair_sum + bias
    flat_grad = cotangent.reshape(row_count * col_count, out_width)
    weight_part = jnp.einsum("pk,pe->ke", half_mean, flat_grad, preferred_element_type=jnp.float32)
    weight_grad = lax.psum(weight_part, ("row", "col", "rep"))
    grad_mean = jnp.einsum("pe,ke->pk", flat_grad, weight, preferred_element_type=jnp.float32) / S
    grad_mean = grad_mean.astype(jnp.bfloat16).reshape(row_count, col_count, C, C)
    left_part = jnp.einsum(
        "ijcd,jsd->isc", grad_mean, right_block, preferred_element_type=jnp.float32
    ).reshape(row_count, -1)
    right_part = jnp.einsum(
        "ijcd,isc->jsd", grad_mean, left_block, preferred_element_type=jnp.float32
    ).reshape(col_count, -1)
    left_sum = lax.psum_scatter(left_part, "col", scatter_dimension=0, tiled=True)
    right_sum = lax.psum_scatter(right_part, "row", scatter_dimension=0, tiled=True)
    return (pair_out, left_sum.astype(jnp.bfloat16), right_sum.astype(jnp.bfloat16), weight_grad)


def exchange(x, axis, flip, size):
    return lax.ppermute(x, axis, [(k, k ^ flip) for k in range(size)])


def swap_blocks(blocks, width):
    count = len(blocks)
    lane_block = lax.broadcasted_iota(jnp.int32, blocks[0].shape, 1) // width
    bit = 1
    while bit < count:
        upper = (lane_block & bit) != 0
        out = list(blocks)
        for a in range(count):
            if a & bit == 0:
                low, high = blocks[a], blocks[a | bit]
                out[a] = jnp.where(upper, pltpu.roll(high, bit * width, 1), low)
                out[a | bit] = jnp.where(upper, high, pltpu.roll(low, LANES - bit * width, 1))
        blocks = out
        bit *= 2
    return blocks


def pick_diagonals(blocks, width, sign):
    count = len(blocks)
    lane_block = lax.broadcasted_iota(jnp.int32, blocks[0].shape, 1) // width
    bit = 1
    while bit < count:
        upper = (lane_block & bit) != 0
        blocks = [jnp.where(upper, blocks[(m + sign * bit) % count], blocks[m]) for m in range(count)]
        bit *= 2
    return blocks


def skew_blocks(blocks, width):
    count = len(blocks)
    blocks = pick_diagonals([pltpu.roll(x, k * width, 1) if k else x for k, x in enumerate(blocks)], width, 1)
    return [blocks[-c % count] for c in range(count)]


def block_kernel(left_in, right_in, cotangent_in, bias_in, block, bias, left, right, cotangent, sems):
    pairs = ((left_in, left), (right_in, right), (cotangent_in, cotangent), (bias_in, bias))
    copies = [pltpu.make_async_copy(source, into, sems.at[k]) for k, (source, into) in enumerate(pairs)]
    for copy in copies:
        copy.start()
    for copy in copies:
        copy.wait()
    held, width = left.shape
    groups = width // LANES
    parts = [ref[t:t + 1, :].astype(F32).reshape(groups, LANES) for ref in (left, right) for t in range(held)]
    turned = jnp.concatenate(pick_diagonals(parts, C, -1), axis=0).T
    parts = pick_diagonals([turned[k * C:(k + 1) * C, :] for k in range(LANES // C)], C, 1)
    rows = [pltpu.roll(parts[-k], LANES - k * C, 1) if k else parts[0] for k in range(len(parts))]
    block[0, :LANES, :] = jnp.concatenate(rows, axis=0).astype(BF16)
    per_row, per_col, _ = cotangent.shape
    cot = cotangent[...].astype(F32)
    parts = [cot[:, j, :] for j in range(per_col)]
    block[0, LANES:, :] = jnp.concatenate(parts, axis=0).astype(BF16)


def turn_back(rows, scratch, left_grad, right_grad):
    held, width = left_grad.shape
    groups = width // LANES
    blocks = swap_blocks([rows[k * C:(k + 1) * C, :] for k in range(LANES // C)], C)
    scratch[...] = jnp.concatenate(blocks, axis=0).T
    for at, ref in ((0, left_grad), (held * groups, right_grad)):
        for g in range(groups):
            ref[:, g * LANES:(g + 1) * LANES] = scratch[pl.ds(at + g, held, stride=groups), :].astype(BF16)


def spread(source, col, slots, first, into, stride):
    for slot in range(slots):
        for t in range(2):
            at = (col ^ slot) * 2 + t
            into[pl.ds(at, C, stride=stride), :] = source[slot, first + t * C:first + (t + 1) * C, :].astype(F32)


def spread_cot(source, col, slots, rows, into):
    per_row = 2 * slots
    for slot in range(slots):
        cot = source[slot, 4 * C:, :].astype(F32)
        for j in range(2 * rows):
            at = pl.multiple_of(((col ^ slot) * 2 + j % 2) * per_row, per_row)
            into[j // 2, pl.ds(at, per_row), :] = cot[j * per_row:(j + 1) * per_row, :]


def mixing_rows(outer_weight, cot_rows):
    tokens = cot_rows[0].shape[0]
    copies = LANES // tokens
    repeated = jnp.concatenate([jnp.concatenate([rows] * copies, axis=0) for rows in cot_rows], axis=0).astype(BF16)
    grads = lax.dot_general(outer_weight, repeated, NT, preferred_element_type=F32)
    copy_of = lax.broadcasted_iota(jnp.int32, (C, LANES), 1) // tokens
    out = []
    for two in range(2):
        lanes = grads[:, two * LANES:(two + 1) * LANES]
        parts = []
        for group in range(C // copies):
            first = group * copies * C
            part = lanes[first:first + C, :]
            for k in range(1, copies):
                at = first + k * C
                part = jnp.where(copy_of == k, lanes[at:at + C, :], part)
            parts.append((part * (1.0 / S)).astype(BF16))
        out.append(jnp.concatenate(parts, axis=1))
    return jnp.concatenate(out, axis=0)


def left_cots(cot, half, col, slots):
    per_row = 2 * slots
    return [cot[half, pl.ds(col * 2 + t, per_row, stride=per_row), :] for t in range(2)]


def right_cots(cot, half, col, slots):
    per_row = 2 * slots
    return [cot[half, pl.ds(pl.multiple_of((col * 2 + t) * per_row, per_row), per_row), :] for t in range(2)]


def near_kernel(rows, near, weight, sent, lefts, cot, grads, far_mix, spread_right, weight_dc):
    slots = near.shape[0]
    row, col = lax.axis_index("row"), lax.axis_index("col")
    tokens = 2 * slots
    spread(near, col, slots, 0, lefts, tokens)
    spread(near, col, slots, 2 * C, spread_right, tokens)
    spread_cot(near, col, slots, rows, cot)
    span = tokens * C
    sent[:span, :] = lefts[...].astype(BF16)
    for slot in range(slots):
        sent[pl.ds(pl.multiple_of(span + (col ^ slot) * 2 * C, 2 * C), 2 * C), :] = near[slot, 2 * C:4 * C, :]
    all_weight = weight[...]
    weight_dc[...] = jnp.swapaxes(all_weight.astype(F32).reshape(C, C, LANES), 0, 1).reshape(C * C, LANES).astype(BF16)
    mix = mixing_rows(weight_dc[...], left_cots(cot, row, col, slots))
    grads[:2 * C, :] = jnp.dot(mix, spread_right[...].astype(BF16), preferred_element_type=F32)
    far_mix[...] = mixing_rows(weight_dc[...], left_cots(cot, 1 - row, col, slots))
    mix = mixing_rows(all_weight, right_cots(cot, row, col, slots))
    grads[2 * C:, :] = jnp.dot(mix, lefts[...].astype(BF16), preferred_element_type=F32)


def ordered(first, near, far):
    return jnp.concatenate([jnp.where(first, near, far), jnp.where(first, far, near)], axis=1)


def far_kernel(
    rows, far, near, near_lefts, near_cot, near_grads, far_mix, weight,
    lefts, rights, cot_all, left_grad, right_grad, far_lefts, far_cot, spread_right, turned,
):
    slots = far.shape[0]
    row, col = lax.axis_index("row"), lax.axis_index("col")
    per_row = 2 * slots
    tokens = rows * per_row
    spread(far, col, slots, 0, far_lefts, per_row)
    spread(far, col, slots, 2 * C, spread_right, per_row)
    spread_cot(far, col, slots, rows, far_cot)
    left = jnp.dot(far_mix[...], spread_right[...].astype(BF16), preferred_element_type=F32)
    mix = mixing_rows(weight[...], right_cots(far_cot, row, col, slots))
    right = jnp.dot(mix, far_lefts[...].astype(BF16), preferred_element_type=F32)
    turn_back(near_grads[...] + jnp.concatenate([left, right], axis=0), turned, left_grad, right_grad)
    first = row == 0
    both = ordered(first, near_lefts[...].reshape(C, per_row, LANES), far_lefts[...].reshape(C, per_row, LANES))
    lefts[...] = both.reshape(C * tokens, LANES).astype(BF16)
    sort_rights(near, far, row, col, slots, rows, 2 * C, rights)
    for q in range(slots):
        at = slice(q * 2 * per_row, (q + 1) * 2 * per_row)
        for half in range(rows):
            near_rows = near_cot[half, at, :].reshape(2, per_row, LANES)
            both = ordered(first, near_rows, far_cot[half, at, :].reshape(2, per_row, LANES))
            first_row = (q * rows + half) * 2 * tokens
            cot_all[first_row:first_row + 2 * tokens, :] = both.reshape(2 * tokens, LANES).astype(BF16)


def sort_rights(near, far, row, col, slots, rows, first, into):
    for half, source in enumerate((near, far)):
        for slot in range(slots):
            chip = (col ^ slot) * rows + lax.rem(row + half, rows)
            into[pl.ds(pl.multiple_of(chip * 2 * C, 2 * C), 2 * C), :] = source[slot, first:first + 2 * C, :]


def outer_kernel(
    rows, slots, near_sent, own_lefts, own_rights, other, cot_all, weight, bias, left_in, right_in,
    pair_out, left_out, right_out, weight_out, spread_left, lefts, rights, pair_block, weight_grad, sems,
):
    row, col, rep = lax.axis_index("row"), lax.axis_index("col"), lax.axis_index("rep")
    copies = [
        pltpu.make_async_copy(left_in, left_out, sems.at[0]),
        pltpu.make_async_copy(right_in, right_out, sems.at[1]),
    ]
    for copy in copies:
        copy.start()
    per_row, per_col = 2 * slots, 2 * rows
    tokens = rows * per_row
    span = per_row * C
    stride = (other.shape[0] - 2 * span) // slots
    for slot in range(slots):
        for t in range(2):
            at = 2 * span + slot * stride + t * C
            spread_left[pl.ds((col ^ slot) * 2 + t, C, stride=per_row), :] = other[at:at + C, :].astype(F32)
    near = other[:span, :].astype(F32).reshape(C, per_row, LANES)
    both = ordered(row == 0, near, spread_left[...].reshape(C, per_row, LANES))
    lefts[rep] = own_lefts[...]
    lefts[1 - rep] = both.reshape(C * tokens, LANES).astype(BF16)
    rights[rep] = own_rights[...]
    for q in range(slots):
        at = pl.multiple_of((q * rows + row) * 2 * C, 2 * C)
        rights[1 - rep, pl.ds(at, 2 * C), :] = other[span + q * 2 * C:span + (q + 1) * 2 * C, :]
        at = pl.multiple_of(((col ^ q) * rows + 1 - row) * 2 * C, 2 * C)
        rights[1 - rep, pl.ds(at, 2 * C), :] = other[2 * span + q * stride + 2 * C:2 * span + q * stride + 4 * C, :]

    def all_of(ref, at):
        return jnp.concatenate([ref[0, at, :], ref[1, at, :]], axis=1)

    right_all = all_of(rights, slice(None))
    count = LANES // tokens
    groups = C // count
    means = [[[] for _ in range(groups)] for _ in range(count)]
    for g in range(groups):
        if g % 2 == 0:
            left = all_of(lefts, slice(g * LANES, (g + 2) * LANES))
            wide = lax.dot_general(right_all, left, NT, preferred_element_type=F32)
        outer = wide[:, g % 2 * LANES:(g % 2 + 1) * LANES]
        for h in range(tokens // count):
            first = h * count * C
            blocks = [outer[first + k * C:first + (k + 1) * C, :] for k in range(count)]
            for c, mean in enumerate(skew_blocks(blocks, tokens)):
                means[c][g].append(mean)
    own_count = per_col // 2
    at = pl.ds(pl.multiple_of((col * per_col + rep * own_count) * C, own_count * C), own_count * C)
    own_left = jnp.concatenate([near_sent[:span, :], other[:span, :]], axis=1)
    own_right = jnp.concatenate([rights[rep, at, :], rights[1 - rep, at, :]], axis=1)
    own = lax.dot_general(own_left, own_right, NT, preferred_element_type=F32) * (1.0 / S)
    own_mean = jnp.concatenate(
        [
            jnp.concatenate([own[c * per_row:(c + 1) * per_row, t * C:(t + 1) * C] for c in range(C)], axis=1)
            for t in range(own_count)
        ],
        axis=0,
    ).astype(BF16)
    own_pairs = jnp.dot(own_mean, weight[...], preferred_element_type=F32) + bias[...]
    for t in range(own_count):
        pair_block[:, t, :] = own_pairs[t * per_row:(t + 1) * per_row, :]
    copy = pltpu.make_async_copy(pair_block, pair_out, sems.at[2])
    copy.start()
    copies.append(copy)
    for c in range(count):
        mean = jnp.concatenate([jnp.concatenate(halves, axis=1) for halves in means[c]], axis=0).astype(BF16)
        cot = jnp.concatenate(
            [
                cot_all[at:at + tokens, :]
                for h in range(tokens // count)
                for at in [(h * count + (k - c) % count) * tokens for k in range(count)]
            ],
            axis=0,
        )
        part = jnp.dot(mean, cot, preferred_element_type=F32) * (1.0 / S)
        at = slice(c * C, (c + 1) * C)
        weight_grad[:, at, :] = part.reshape(groups, C, LANES)
        copy = pltpu.make_async_copy(weight_grad.at[:, at], weight_out.at[:, at], sems.at[3 + c])
        copy.start()
        copies.append(copy)

    for copy in copies:
        copy.wait()


def gather_plan(rows, cols, left_features, right_features, weight, bias, cotangent):
    held, width = left_features.shape
    seqs = width // C
    tokens = held * rows * cols
    half_span = tokens // rows * C
    per_row, per_col, e = cotangent.shape
    vmem = pl.BlockSpec(memory_space=pltpu.VMEM)
    anywhere = pl.BlockSpec(memory_space=pl.ANY)
    params = pltpu.CompilerParams(vmem_limit_bytes=32 * 1024 * 1024)
    array = jax.ShapeDtypeStruct

    in_hbm = [left_features, right_features, cotangent, bias.reshape(1, e)]
    block, bias_row = pl.pallas_call(
        block_kernel,
        out_shape=(array((1, 2 * held * C + per_row * per_col, seqs), BF16), array((1, e), F32)),
        in_specs=[pl.BlockSpec(memory_space=pltpu.HBM)] * 4,
        out_specs=(vmem, vmem),
        scratch_shapes=[
            pltpu.VMEM((held, width), BF16),
            pltpu.VMEM((held, width), BF16),
            pltpu.VMEM((per_row, per_col, e), BF16),
            pltpu.SemaphoreType.DMA((4,)),
        ],
        compiler_params=params,
        name="own_block",
    )(*(pltpu.with_memory_space_constraint(x, pltpu.HBM) for x in in_hbm))
    flip = 1
    while flip < cols:
        arrived = exchange(block, "col", flip, cols)
        if flip * 2 == cols:
            far = [exchange(block, "row", 1, rows), exchange(arrived, "row", 1, rows)]
        block = jnp.concatenate([block, arrived], axis=0)
        flip *= 2
    far = jnp.concatenate(far, axis=0)

    lefts = array((half_span, seqs), F32)
    cots = array((rows, cols * held * per_row, e), F32)
    near_sent, near_lefts, near_cot, near_grads, far_mix = pl.pallas_call(
        functools.partial(near_kernel, rows),
        out_shape=(
            array((2 * half_span, seqs), BF16),
            lefts,
            cots,
            array((2 * held * C, seqs), F32),
            array((held * C, half_span), BF16),
        ),
        in_specs=[vmem] * 2,
        out_specs=(vmem,) * 5,
        scratch_shapes=[pltpu.VMEM((half_span, seqs), F32), pltpu.VMEM((C * C, e), BF16)],
        compiler_params=params,
        cost_estimate=pl.CostEstimate(flops=300_000_000, bytes_accessed=2_000_000, transcendentals=0),
        name="near_part",
    )(block, weight)
    other = exchange(jnp.concatenate([near_sent, far[:, :2 * held * C].reshape(-1, seqs)], axis=0), "rep", 1, 2)

    own_lefts, own_rights, cot_all, left_grad, right_grad = pl.pallas_call(
        functools.partial(far_kernel, rows),
        out_shape=(
            array((tokens * C, seqs), BF16),
            array((tokens * C, seqs), BF16),
            array((tokens * tokens, e), BF16),
            array((held, width), BF16),
            array((held, width), BF16),
        ),
        in_specs=[vmem] * 7,
        out_specs=(vmem,) * 5,
        scratch_shapes=[
            pltpu.VMEM((half_span, seqs), F32),
            pltpu.VMEM(cots.shape, F32),
            pltpu.VMEM((half_span, seqs), F32),
            pltpu.VMEM((LANES, LANES), F32),
        ],
        compiler_params=params,
        cost_estimate=pl.CostEstimate(flops=10_000_000_000, bytes_accessed=1_000_000, transcendentals=0),
        name="far_part",
    )(far, block, near_lefts, near_cot, near_grads, far_mix, weight)

    split = (C * tokens // LANES, LANES // tokens * C, e)
    pair_out, left_grad, right_grad, weight_grad = pl.pallas_call(
        functools.partial(outer_kernel, rows, cols),
        out_shape=(
            array((per_row, per_col // 2, e), F32),
            array((held, width), BF16),
            array((held, width), BF16),
            array(split, F32),
        ),
        in_specs=[vmem] * 9,
        out_specs=(anywhere,) * 4,
        scratch_shapes=[
            pltpu.VMEM((half_span, seqs), F32),
            pltpu.VMEM((2, tokens * C, seqs), BF16),
            pltpu.VMEM((2, tokens * C, seqs), BF16),
            pltpu.VMEM((per_row, per_col // 2, e), F32),
            pltpu.VMEM(split, F32),
            pltpu.SemaphoreType.DMA((3 + LANES // tokens,)),
        ],
        compiler_params=params,
        name="outer_mean",
    )(near_sent, own_lefts, own_rights, other, cot_all, weight, bias_row, left_grad, right_grad)
    return pair_out, left_grad, right_grad, weight_grad.reshape(C * C, e)


def solution(mesh):
    rows, cols = mesh.shape["row"], mesh.shape["col"]

    def on_device(left_features, right_features, weight, bias, cotangent):
        held, width = left_features.shape
        tokens = held * rows * cols
        small = held == 2 and rows == 2 and cols & (cols - 1) == 0 and LANES % tokens == 0 and tokens == 16
        if small and width == LANES * C and weight.shape[1] == LANES and C % (LANES // tokens) == 0:
            return gather_plan(rows, cols, left_features, right_features, weight, bias, cotangent)
        return tile_plan(left_features, right_features, weight, bias, cotangent)

    in_specs = (
        P(("groups", "row", "col"), "rep"),
        P(("groups", "col", "row"), "rep"),
        P(),
        P(),
        P(("groups", "row"), "col", None),
    )
    out_specs = (
        P(("groups", "row"), ("col", "rep"), None),
        P(("groups", "row", "col"), "rep"),
        P(("groups", "col", "row"), "rep"),
        P("groups", None),
    )
    return jax.shard_map(
        on_device, mesh=mesh, in_specs=in_specs, out_specs=out_specs, check_vma=False
    )
```
